128 devices in a mesh: blk: 8 (over y_lo, x), grp: 16 (over y_hi, z, core).
Axes of the slice: x: 4, y: 4 (y_hi: 2, y_lo: 2; y = y_hi * 2 + y_lo), z: 4, core: 2. Of those that a mesh axis runs over, the one named last changes fastest.
Arguments:
- queries: bfloat16 [2048, 4096], P(('blk', 'grp')), may hold values from -2 to 2
- document_vectors: bfloat16 [2048, 4096], P(('blk', 'grp')), may hold values from -1.5 to 1.5
- negatives: bfloat16 [8192, 4096], P(('blk', 'grp')), may hold values from -1.5 to 1.5
- positives: int32 [2048], P(('blk', 'grp')), may hold values from 0 to 2047
- neg_ids: int32 [2048, 7], P(('blk', 'grp')), may hold values from 0 to 8191, as said below
Outputs:
- grad_queries: bfloat16 [2048, 4096], P(('blk', 'grp'))
- grad_passages: bfloat16 [2048, 4096], P(('blk', 'grp'))
- grad_negatives: bfloat16 [8192, 4096], P(('blk', 'grp'))
The draws below stay inside these ranges and needn't reach their ends.
Inputs may be any that keep to these rules, and one draw needn't show every extreme that they name: `neg_ids`: row i holds the 7 negatives of query i as indices into negatives; the owner device of index n is n // 64. In the aligned blocks of 16 rows (the queries of one device) no owner device is named more than 2 times, and some owner exactly 2 times.
All inputs are finite; a program needn't handle non-finite values.
Results may differ from the reference program's by a relative error of at most 0.02.
Values may be sent and summed in bfloat16 or wider, within the bound.
A program may use at most 64 MiB of HBM per device.

```python
import math
import jax
import jax.numpy as jnp
from jax import lax

D = 4096
Q_DEV = 16
HARD = 7
NEG_DEV = 64
QUERIES = 2048
NEGS = 8192
CAP = 2
FULL = 28
N_BLK = 8
N_GRP = 16
DEVICES = 128


def shared_rows(key):
    return jnp.clip(jax.random.normal(jax.random.fold_in(key, 101), (QUERIES, D), jnp.float32), -6.0, 6.0)


def common_direction(key):
    return jnp.clip(jax.random.normal(jax.random.fold_in(key, 202), (D,), jnp.float32), -6.0, 6.0)


def row_scales(key, lowest, highest):
    return jnp.exp(jax.random.uniform(key, (QUERIES, 1), jnp.float32, math.log(lowest), math.log(highest)))


def draw_document_vectors(key, part):
    base_rows = shared_rows(key)
    key = jax.random.fold_in(key, 3)
    scale_key = jax.random.fold_in(key, 0)
    result = base_rows * row_scales(scale_key, 0.5, 2.0) / math.sqrt(D)
    return jnp.clip(result, -1.5, 1.5).astype(jnp.bfloat16)


def draw_queries(key, part):
    direction = common_direction(key)
    key = jax.random.fold_in(key, 5)
    scale_key, own_key = jax.random.split(key, 2)
    own_rows = jnp.clip(jax.random.normal(own_key, (QUERIES, D), jnp.float32), -6.0, 6.0)
    result = row_scales(scale_key, 0.5, 5.0) * (0.8 * own_rows + 0.6 * direction) / math.sqrt(D)
    return jnp.clip(result, -2.0, 2.0).astype(jnp.bfloat16)


def draw_negatives(key, part):
    direction = common_direction(key)
    key = jax.random.fold_in(key, 7)
    shared_weight = 9.6 / math.sqrt(D)
    own_rows = jnp.clip(jax.random.normal(key, (NEGS, D), jnp.float32), -6.0, 6.0)
    result = (own_rows + shared_weight * direction) / math.sqrt(D)
    return jnp.clip(result, -1.5, 1.5).astype(jnp.bfloat16)


def draw_neg_ids(key, part):
    key = jax.random.fold_in(key, 9)
    entries = Q_DEV * HARD
    least = max(1, FULL // 2)

    def one_block(block_key):
        owner_key, count_key, shuffle_key, local_key = jax.random.split(block_key, 4)
        owners = jax.random.permutation(owner_key, DEVICES).astype(jnp.int32)
        full_count = jax.random.randint(count_key, (), least, FULL + 1)
        entry_index = jnp.arange(entries, dtype=jnp.int32)
        spread = (entry_index - full_count * CAP) % (DEVICES - full_count)
        chosen = jnp.where(entry_index < full_count * CAP, entry_index // CAP, full_count + spread)
        owner_dev = owners[chosen]
        shuffle = jax.random.permutation(shuffle_key, entries)
        owner_dev = owner_dev[shuffle]
        local_ids = jax.random.randint(local_key, (entries,), 0, NEG_DEV)
        return (owner_dev * NEG_DEV + local_ids).reshape(Q_DEV, HARD)
    block_keys = jax.random.split(key, DEVICES)
    return jax.vmap(one_block)(block_keys).reshape(QUERIES, HARD).astype(jnp.int32)


def plant(values, key, low, high):
    spot = [jax.random.randint(jax.random.fold_in(key, axis), (), 0, length) for axis, length in enumerate(values.shape)]
    longest = values.shape.index(max(values.shape))
    neighbour = spot[:longest] + [(spot[longest] + 1) % values.shape[longest]] + spot[longest + 1:]
    return values.at[tuple(spot)].set(low).at[tuple(neighbour)].set(high)


def setup_inputs(seed: int = 0) -> dict:
    keys = jax.random.split(jax.random.key(seed), 6)
    queries = draw_queries(jax.random.fold_in(keys[5], 71), 0)
    document_vectors = draw_document_vectors(jax.random.fold_in(keys[5], 71), 0)
    negatives = draw_negatives(jax.random.fold_in(keys[5], 71), 0)
    positives = plant(jax.random.randint(keys[3], (QUERIES,), 0, QUERIES), jax.random.fold_in(keys[3], 1), 0, QUERIES - 1).astype(jnp.int32)
    neg_ids = draw_neg_ids(jax.random.fold_in(keys[5], 71), 0)
    return {"queries": queries, "document_vectors": document_vectors, "negatives": negatives, "positives": positives, "neg_ids": neg_ids}


sharpness_divisor = 0.02


def reference(queries, document_vectors, negatives, positives, neg_ids):
    block_rows = Q_DEV * N_GRP
    grouped = document_vectors.reshape(N_BLK, N_GRP, Q_DEV, D)
    by_group = jnp.transpose(grouped, (1, 0, 2, 3)).reshape(N_GRP, N_BLK * Q_DEV, D)
    columns = jnp.arange(QUERIES, dtype=jnp.int32)

    def add_part(running, contraction_operands):
        pairwise_dot_value = jnp.dot(contraction_operands[0], contraction_operands[1], preferred_element_type=jnp.float32) / sharpness_divisor
        return running + lax.optimization_barrier(pairwise_dot_value.astype(jnp.bfloat16)).astype(jnp.float32), None

    def one_block(carried, inputs):
        grad_pass, grad_negs = carried
        question_slab_height, pos_block, id_block = inputs
        affinity_matrix = jnp.dot(question_slab_height, document_vectors.T, preferred_element_type=jnp.float32) / sharpness_divisor
        distractor_slab = negatives[id_block]
        mined_distractor_scaled_scores = jnp.einsum("jy,jiy->ji", question_slab_height.astype(jnp.float32), distractor_slab.astype(jnp.float32)) / sharpness_divisor
        highest = jnp.maximum(jnp.max(affinity_matrix, 1), jnp.max(mined_distractor_scaled_scores, 1))
        summed = jnp.sum(jnp.exp(affinity_matrix - highest[:, None]), 1) + jnp.sum(jnp.exp(mined_distractor_scaled_scores - highest[:, None]), 1)
        log_total = highest + jnp.log(summed)
        target = (columns[None, :] == pos_block[:, None]).astype(jnp.float32)
        normalized_likelihoods = (jnp.exp(affinity_matrix - log_total[:, None]) - target).astype(jnp.bfloat16)
        mined_distractor_likelihoods = jnp.exp(mined_distractor_scaled_scores - log_total[:, None]).astype(jnp.bfloat16)
        w_groups = jnp.transpose(normalized_likelihoods.reshape(block_rows, N_BLK, N_GRP, Q_DEV), (2, 0, 1, 3))
        w_groups = w_groups.reshape(N_GRP, block_rows, N_BLK * Q_DEV)
        batch_part, _ = lax.scan(add_part, jnp.zeros((block_rows, D), jnp.float32), (w_groups, by_group))
        mined_distractor_share = jnp.einsum("he,her->hr", mined_distractor_likelihoods.astype(jnp.float32), distractor_slab.astype(jnp.float32)) / sharpness_divisor
        grad_block = (batch_part + mined_distractor_share).astype(jnp.bfloat16)
        objective_term_value = jnp.dot(normalized_likelihoods.T, question_slab_height, preferred_element_type=jnp.float32) / sharpness_divisor
        grad_pass = grad_pass + lax.optimization_barrier(objective_term_value.astype(jnp.bfloat16)).astype(jnp.float32)
        mined_distractor_grads = (mined_distractor_likelihoods.astype(jnp.float32)[:, :, None] * question_slab_height.astype(jnp.float32)[:, None, :]) / sharpness_divisor
        mined_distractor_grads = lax.optimization_barrier(mined_distractor_grads.astype(jnp.bfloat16)).astype(jnp.float32)
        grad_negs = grad_negs + jax.ops.segment_sum(mined_distractor_grads.reshape(block_rows * HARD, D), id_block.reshape(block_rows * HARD), num_segments=NEGS)
        return (grad_pass, grad_negs), grad_block

    start = (jnp.zeros((QUERIES, D), jnp.float32), jnp.zeros((NEGS, D), jnp.float32))
    inputs = (queries.reshape(N_BLK, block_rows, D), positives.reshape(N_BLK, block_rows), neg_ids.reshape(N_BLK, block_rows, HARD))
    (grad_pass, grad_negs), grad_blocks = lax.scan(one_block, start, inputs)
    return grad_blocks.reshape(QUERIES, D), grad_pass.astype(jnp.bfloat16), grad_negs.astype(jnp.bfloat16)
```

```python
import jax
import jax.numpy as jnp
from jax import lax
from jax.experimental import pallas as pl
from jax.experimental.pallas import tpu as pltpu
from jax.sharding import PartitionSpec as P

MESH = pl.DeviceIdType.MESH
BF = jnp.bfloat16
F32 = jnp.float32
INV = 50.0
D = 4096
EXT = 128
NEG = 64
ROWS = 16
COLS = NEG + ROWS
CH = 1024
NF = D // CH
FLOOR = -1e30


def kernel(
    q_in, p_in, n_in, e_in, oq, op, on,
    Q, C, S, W, MU, sibs, ownq, rsib, G, rB, T, rA, g3, g12, gsend, g0, rx2, rf1, rf2, st1, st2,
    lsem, sx, rx, sq, rq, sst, rst1, rst2, sg, rg2, rgf1, rgf2, ssib, rsibs, sB, rBs, sA, rAs,
):
    b_id = lax.axis_index("blk")
    g_id = lax.axis_index("grp")
    x = b_id % 4
    y = (g_id // 8) * 2 + b_id // 4
    z = (g_id // 2) % 4
    c = g_id % 2

    def dev(xx, yy, zz, cc):
        xx, yy, zz = (xx + 4) % 4, (yy + 4) % 4, (zz + 4) % 4
        return {"blk": (yy % 2) * 4 + xx, "grp": ((yy // 2) * 4 + zz) * 2 + cc}

    right, left, sib = dev(x + 1, y, z, c), dev(x - 1, y, z, c), dev(x, y, z, 1 - c)
    A = z + c * (y - z)
    B = y + c * (z - y)

    def at(a, b):
        a, b = (a + 4) % 4, (b + 4) % 4
        return dev(x, b + c * (a - b), a + c * (b - a), c)

    def slot(cc, b, a):
        return cc * 16 + ((b + 4) % 4) * 4 + (a + 4) % 4

    def rows_of(s, count=ROWS):
        return pl.ds(pl.multiple_of(s * ROWS, ROWS), count)

    sent = []

    def send(src, dst, ss, rs, to):
        cp = pltpu.make_async_remote_copy(
            src_ref=src, dst_ref=dst, send_sem=ss, recv_sem=rs, device_id=to, device_id_type=MESH
        )
        cp.start()
        sent.append(cp)

    def arrived(dst, rs):
        pltpu.make_async_remote_copy(
            src_ref=dst, dst_ref=dst, send_sem=lsem.at[0], recv_sem=rs, device_id=sib, device_id_type=MESH
        ).wait_recv()

    mine = slot(c, B, A)
    own_rows = rows_of(mine)
    local = [
        pltpu.make_async_copy(n_in, C.at[pl.ds(0, NEG)], lsem.at[0]),
        pltpu.make_async_copy(p_in, C.at[pl.ds(NEG, ROWS)], lsem.at[1]),
        pltpu.make_async_copy(q_in, Q.at[own_rows, pl.ds(0, D)], lsem.at[2]),
        pltpu.make_async_copy(e_in, Q.at[own_rows, pl.ds(D, EXT)], lsem.at[3]),
    ]
    for cp in local:
        cp.start()
    barrier = pltpu.get_barrier_semaphore()
    greet = [right, left, sib]
    greet += [dev(x, y + dy, z, cc) for dy in (1, 2, 3) for cc in (0, 1)]
    greet += [dev(x, y, z + dz, c) for dz in (1, 2, 3)]
    for to in greet:
        pl.semaphore_signal(barrier, inc=1, device_id=to, device_id_type=MESH)
    for cp in local:
        cp.wait()
    pl.semaphore_wait(barrier, len(greet))

    def fcols(f):
        return pl.ds(f * CH, CH)

    def crows(k):
        return pl.ds(k * COLS, COLS)

    for i in range(NF):
        f, h = i, (i + 2) % 4
        send(C.at[crows(0), fcols(f)], C.at[crows(1), fcols(f)], sx.at[0, f], rx.at[0, f], right)
        send(C.at[crows(0), fcols(h)], C.at[crows(2), fcols(h)], sx.at[1, h], rx.at[1, h], left)
    for da in (1, 3, 2):
        send(Q.at[own_rows], Q.at[own_rows], sq.at[0, da], rq.at[mine], at(A + da, B))

    def spread(s):
        da = s
        r = slot(c, B, A - da)
        rr = rows_of(r)
        if da:
            arrived(Q.at[rr], rq.at[r])
        for db in (1, 3, 2):
            send(Q.at[rr], Q.at[rr], sq.at[1 + da, db], rq.at[r], at(A, B + db))
        send(Q.at[rr], Q.at[rr], sq.at[1 + da, 0], rq.at[r], sib)

    for da in (0, 1, 3, 2):
        spread(da)
    for f in (0, 1):
        arrived(C.at[crows(1), fcols(f)], rx.at[0, f])
        send(C.at[crows(1), fcols(f)], C.at[crows(3), fcols(f)], sx.at[2, f], rx.at[2, f], right)
        h = f + 2
        arrived(C.at[crows(2), fcols(h)], rx.at[1, h])
        send(C.at[crows(2), fcols(h)], C.at[crows(3), fcols(h)], sx.at[2, h], rx.at[2, h], left)
    for da in (0, 1, 3, 2):
        for db in (1, 3, 2):
            r = slot(c, B - db, A - da)
            rr = rows_of(r)
            arrived(Q.at[rr], rq.at[r])
            send(Q.at[rr], Q.at[rr], sq.at[4 + db, da], rq.at[r], sib)
    for k in range(16):
        r = (1 - c) * 16 + k
        arrived(Q.at[rows_of(r)], rq.at[r])

    ext = jnp.transpose(Q[:, D : D + EXT].astype(F32))
    ids = ext[0:8] * 128.0 + ext[8:16]
    col_neg = lax.broadcasted_iota(jnp.int32, (NEG, 512), 0)
    col_pas = lax.broadcasted_iota(jnp.int32, (ROWS, 512), 0)
    for k, dx in enumerate((0, 3, 1, 2)):
        lin = ((y % 2) * 4 + (x + dx) % 4) * 16 + g_id
        gid = (col_neg + lin * NEG).astype(F32)
        mult = jnp.zeros((NEG, 512), F32)
        for h in range(7):
            mult = mult + (ids[h : h + 1] == gid).astype(F32)
        MU[k * COLS : k * COLS + NEG, :] = mult
        pid = (col_pas + lin * ROWS).astype(F32)
        MU[k * COLS + NEG : (k + 1) * COLS, :] = (ids[7:8] == pid).astype(F32)

    def scores(lo, hi):
        S[lo:hi, :] = INV * lax.dot_general(
            C[lo:hi, :], Q[:, 0:D], (((1,), (1,)), ((), ())), preferred_element_type=F32
        )
        for k in range(lo // COLS, hi // COLS):
            r0, r1 = k * COLS, k * COLS + NEG
            S[r0:r1, :] = jnp.where(MU[r0:r1, :] > 0.0, S[r0:r1, :], FLOOR)

    for f in (2, 3):
        arrived(C.at[crows(1), fcols(f)], rx.at[0, f])
        arrived(C.at[crows(2), fcols(f - 2)], rx.at[1, f - 2])
    scores(0, 3 * COLS)
    for f in (0, 2, 1, 3):
        arrived(C.at[crows(3), fcols(f)], rx.at[2, f])
    scores(3 * COLS, 4 * COLS)

    s_all = S[...]
    m = jnp.max(s_all, 0, keepdims=True)
    e = jnp.exp(s_all - m)
    tot = jnp.zeros((1, 512), F32)
    for k in range(4):
        r0, r1, r2 = k * COLS, k * COLS + NEG, (k + 1) * COLS
        tot = tot + jnp.sum(e[r0:r1] * MU[r0:r1, :], 0, keepdims=True)
        tot = tot + jnp.sum(e[r1:r2], 0, keepdims=True)
    for j in range(4):
        st1[0, j : j + 1, :] = m[:, j * 128 : (j + 1) * 128]
        st1[0, 4 + j : 5 + j, :] = tot[:, j * 128 : (j + 1) * 128]

    def merge(buf, n):
        top = buf[0, 0:4, :]
        for i in range(1, n):
            top = jnp.maximum(top, buf[i, 0:4, :])
        total = jnp.zeros((4, 128), F32)
        for i in range(n):
            total = total + buf[i, 4:8, :] * jnp.exp(buf[i, 0:4, :] - top)
        return top, total

    for i in range(1, 8):
        dy, dc = i // 2, i % 2
        send(st1.at[0], st1.at[i], sst.at[i], rst1.at[i], dev(x, y + dy, z, (c + dc) % 2))
    for i in range(1, 8):
        arrived(st1.at[i], rst1.at[i])
    top, total = merge(st1, 8)
    st2[0, 0:4, :] = top
    st2[0, 4:8, :] = total
    for i in range(1, 4):
        send(st2.at[0], st2.at[i], sst.at[7 + i], rst2.at[i], dev(x, y, z + i, c))
    for i in range(1, 4):
        arrived(st2.at[i], rst2.at[i])
    top, total = merge(st2, 4)
    lt = top + jnp.log(total)
    log_total = jnp.concatenate([lt[j : j + 1, :] for j in range(4)], 1)

    def weights(k):
        r0, r1, r2 = k * COLS, k * COLS + NEG, (k + 1) * COLS
        hard = jnp.exp(S[r0:r1, :] - log_total).astype(BF).astype(F32) * MU[r0:r1, :]
        W[r0:r1, :] = hard.astype(BF)
        W[r1:r2, :] = (jnp.exp(S[r1:r2, :] - log_total) - MU[r1:r2, :]).astype(BF)

    def col_grad(lo, hi, f):
        return INV * jnp.dot(W[lo:hi, :], Q[:, f * CH : (f + 1) * CH], preferred_element_type=F32)

    weights(3)
    for f in (0, 2, 1, 3):
        g3[:, f * CH : (f + 1) * CH] = col_grad(3 * COLS, 4 * COLS, f).astype(BF)
        to = right if f < 2 else left
        send(g3.at[:, fcols(f)], rx2.at[:, fcols(f)], sg.at[0, f], rg2.at[f], to)
    for k in (0, 1, 2):
        weights(k)

    def query_grad(core, f):
        w = W[:, pl.ds(pl.multiple_of(core * 256, 256), 256)]
        return INV * lax.dot_general(
            w, C[:, f * CH : (f + 1) * CH], (((0,), (0,)), ((), ())), preferred_element_type=F32
        )

    for f in range(NF):
        sibs[:, f * CH : (f + 1) * CH] = query_grad(1 - c, f).astype(BF)
        send(sibs.at[:, fcols(f)], rsib.at[:, fcols(f)], ssib.at[f], rsibs.at[f], sib)
    for f in range(NF):
        cs = slice(f * CH, (f + 1) * CH)
        g12[:, cs] = col_grad(COLS, 3 * COLS, f)
        if f < 2:
            gsend[0:COLS, cs] = g12[0:COLS, cs].astype(BF)
            send(gsend.at[pl.ds(0, COLS), fcols(f)], rf2.at[:, fcols(f)], sg.at[1, f], rgf2.at[f], left)
        else:
            gsend[COLS:, cs] = g12[COLS:, cs].astype(BF)
            send(gsend.at[pl.ds(COLS, COLS), fcols(f)], rf1.at[:, fcols(f)], sg.at[1, f], rgf1.at[f], right)
    for f in range(NF):
        ownq[:, f * CH : (f + 1) * CH] = query_grad(c, f)
    for f in range(NF):
        cs = slice(f * CH, (f + 1) * CH)
        arrived(rsib.at[:, fcols(f)], rsibs.at[f])
        G[:, cs] = (ownq[:, cs] + rsib[:, cs].astype(F32)).astype(BF)
        for db in (2, 1, 3):
            src = G.at[rows_of(slot(0, B + db, 0), 64), fcols(f)]
            send(src, rB.at[db, :, fcols(f)], sB.at[db, f], rBs.at[db, f], at(A, B + db))
    for f in (0, 2, 1, 3):
        cs = slice(f * CH, (f + 1) * CH)
        arrived(rx2.at[:, fcols(f)], rg2.at[f])
        if f < 2:
            gsend[COLS:, cs] = (g12[COLS:, cs] + rx2[:, cs].astype(F32)).astype(BF)
            send(gsend.at[pl.ds(COLS, COLS), fcols(f)], rf1.at[:, fcols(f)], sg.at[2, f], rgf1.at[f], right)
        else:
            gsend[0:COLS, cs] = (g12[0:COLS, cs] + rx2[:, cs].astype(F32)).astype(BF)
            send(gsend.at[pl.ds(0, COLS), fcols(f)], rf2.at[:, fcols(f)], sg.at[2, f], rgf2.at[f], left)
    for f in range(NF):
        g0[:, f * CH : (f + 1) * CH] = col_grad(0, COLS, f)
    for f in range(NF):
        cs = slice(f * CH, (f + 1) * CH)
        t = G[rows_of(slot(0, B, 0), 64), cs].astype(F32)
        for db in (1, 2, 3):
            arrived(rB.at[db, :, fcols(f)], rBs.at[db, f])
            t = t + rB[db, :, cs].astype(F32)
        T[:, cs] = t.astype(BF)
        for da in (2, 1, 3):
            src = T.at[rows_of(slot(0, 0, A + da)), fcols(f)]
            send(src, rA.at[da, :, fcols(f)], sA.at[da, f], rAs.at[da, f], at(A + da, B))
    for f in range(NF):
        cs = slice(f * CH, (f + 1) * CH)
        t = T[rows_of(A), cs].astype(F32)
        for da in (1, 2, 3):
            arrived(rA.at[da, :, fcols(f)], rAs.at[da, f])
            t = t + rA[da, :, cs].astype(F32)
        oq[:, cs] = t.astype(BF)
    for f in (2, 0, 3, 1):
        cs = slice(f * CH, (f + 1) * CH)
        arrived(rf1.at[:, fcols(f)], rgf1.at[f])
        arrived(rf2.at[:, fcols(f)], rgf2.at[f])
        t = g0[:, cs] + rf1[:, cs].astype(F32) + rf2[:, cs].astype(F32)
        on[:, cs] = t[0:NEG].astype(BF)
        op[:, cs] = t[NEG:COLS].astype(BF)
    for cp in sent:
        cp.wait_send()


def on_device(queries, document_vectors, negatives, positives, neg_ids):
    ids = jnp.concatenate([neg_ids, positives[:, None]], 1)
    pad = jnp.zeros((ROWS, EXT - 16), jnp.int32)
    ext = jnp.concatenate([ids // 128, ids % 128, pad], 1).astype(BF)
    dma = pltpu.SemaphoreType.DMA
    vm = pltpu.VMEM
    return pl.pallas_call(
        kernel,
        out_shape=(
            jax.ShapeDtypeStruct((ROWS, D), BF),
            jax.ShapeDtypeStruct((ROWS, D), BF),
            jax.ShapeDtypeStruct((NEG, D), BF),
        ),
        in_specs=[pl.BlockSpec(memory_space=pl.ANY)] * 4,
        out_specs=tuple([pl.BlockSpec(memory_space=pltpu.VMEM)] * 3),
        scratch_shapes=[
            vm((512, D + EXT), BF),
            vm((4 * COLS, D), BF),
            vm((4 * COLS, 512), F32),
            vm((4 * COLS, 512), BF),
            vm((4 * COLS, 512), F32),
            vm((256, D), BF),
            vm((256, D), F32),
            vm((256, D), BF),
            vm((256, D), BF),
            vm((4, 64, D), BF),
            vm((64, D), BF),
            vm((4, ROWS, D), BF),
            vm((COLS, D), BF),
            vm((2 * COLS, D), F32),
            vm((2 * COLS, D), BF),
            vm((COLS, D), F32),
            vm((COLS, D), BF),
            vm((COLS, D), BF),
            vm((COLS, D), BF),
            vm((8, 8, 128), F32),
            vm((4, 8, 128), F32),
            dma((4,)),
            dma((3, NF)),
            dma((3, NF)),
            dma((8, 4)),
            dma((32,)),
            dma((11,)),
            dma((8,)),
            dma((4,)),
            dma((3, NF)),
            dma((NF,)),
            dma((NF,)),
            dma((NF,)),
            dma((NF,)),
            dma((NF,)),
            dma((4, NF)),
            dma((4, NF)),
            dma((4, NF)),
            dma((4, NF)),
        ],
        compiler_params=pltpu.CompilerParams(
            collective_id=0, has_side_effects=True, vmem_limit_bytes=56 * 2**20
        ),
    )(queries, document_vectors, negatives, ext)


def solution(mesh):
    rows = P(("blk", "grp"), None)
    return jax.shard_map(
        on_device,
        mesh=mesh,
        in_specs=(rows, rows, rows, P(("blk", "grp")), rows),
        out_specs=(rows, rows, rows),
        check_vma=False,
    )
```

```python
import jax
import jax.numpy as jnp
from jax import lax
from jax.experimental import pallas as pl
from jax.experimental.pallas import tpu as pltpu
from jax.sharding import PartitionSpec as P

MESH = pl.DeviceIdType.MESH
BF = jnp.bfloat16
F32 = jnp.float32
INV = 50.0
D = 4096
EXT = 128
NEG = 64
ROWS = 16
COLS = NEG + ROWS
CH = 1024
NF = D // CH
FLOOR = -1e30


def kernel(
    q_in, p_in, n_in, pos_in, ids_in, out,
    PO, ID, E, Q, C, S, W, MU, sibs, ownq, rsib, G, rB2, gB, rB, T, rA, g3, g12, gsend, g0, rx2, rf1, rf2, st1, st2,
    lsem, sx, rx, sq, ssq, rq, sst, rst1, rst2, sg, rg2, rgf1, rgf2, ssib, rsibs, sB, rB2s, rBs, sA, rAs,
):
    b_id = lax.axis_index("blk")
    g_id = lax.axis_index("grp")
    x = b_id % 4
    y = (g_id // 8) * 2 + b_id // 4
    z = (g_id // 2) % 4
    c = g_id % 2

    def dev(xx, yy, zz, cc):
        xx, yy, zz = (xx + 4) % 4, (yy + 4) % 4, (zz + 4) % 4
        return {"blk": (yy % 2) * 4 + xx, "grp": ((yy // 2) * 4 + zz) * 2 + cc}

    right, left, sib = dev(x + 1, y, z, c), dev(x - 1, y, z, c), dev(x, y, z, 1 - c)
    A = z + c * (y - z)
    B = y + c * (z - y)

    def at(a, b):
        a, b = (a + 4) % 4, (b + 4) % 4
        return dev(x, b + c * (a - b), a + c * (b - a), c)

    def slot(cc, b, a):
        return cc * 16 + ((b + 4) % 4) * 4 + (a + 4) % 4

    def rows_of(s, count=ROWS):
        return pl.ds(pl.multiple_of(s * ROWS, ROWS), count)

    sent = []

    def send(src, dst, ss, rs, to):
        cp = pltpu.make_async_remote_copy(
            src_ref=src, dst_ref=dst, send_sem=ss, recv_sem=rs, device_id=to, device_id_type=MESH
        )
        cp.start()
        sent.append(cp)

    def arrived(dst, rs):
        pltpu.make_async_remote_copy(
            src_ref=dst, dst_ref=dst, send_sem=lsem.at[0], recv_sem=rs, device_id=sib, device_id_type=MESH
        ).wait_recv()

    mine = slot(c, B, A)
    own_rows = rows_of(mine)
    local = [
        pltpu.make_async_copy(n_in, C.at[pl.ds(0, NEG)], lsem.at[0]),
        pltpu.make_async_copy(p_in, C.at[pl.ds(NEG, ROWS)], lsem.at[1]),
        pltpu.make_async_copy(q_in, Q.at[own_rows, pl.ds(0, D)], lsem.at[2]),
        pltpu.make_async_copy(pos_in, PO, lsem.at[3]),
        pltpu.make_async_copy(ids_in, ID, lsem.at[4]),
    ]
    for cp in local:
        cp.start()
    barrier = pltpu.get_barrier_semaphore()
    greet = [dev(x, y + dy, z, cc) for dy in (2, 1, 3) for cc in (0, 1)]
    greet += [dev(x, y, z + dz, c) for dz in (2, 1, 3)]
    greet += [right, left, sib]
    for to in greet:
        pl.semaphore_signal(barrier, inc=1, device_id=to, device_id_type=MESH)
    E[...] = jnp.zeros((128, 128), F32)
    for cp in local:
        cp.wait()
    for r, part in ((0, ID[...]), (7, PO[...])):
        n = part.shape[0]
        E[r : r + n, 0:ROWS] = (part // 128).astype(F32)
        E[8 + r : 8 + r + n, 0:ROWS] = (part % 128).astype(F32)
    Q[own_rows, D : D + EXT] = jnp.transpose(E[...])[0:ROWS].astype(BF)
    pl.semaphore_wait(barrier, len(greet))

    def fcols(f):
        return pl.ds(f * CH, CH)

    def crows(k):
        return pl.ds(k * COLS, COLS)

    for i in range(NF):
        f, h = i, (i + 2) % 4
        send(C.at[crows(0), fcols(f)], C.at[crows(1), fcols(f)], sx.at[0, f], rx.at[0, f], right)
        send(C.at[crows(0), fcols(h)], C.at[crows(2), fcols(h)], sx.at[1, h], rx.at[1, h], left)
    for da in (1, 3, 2):
        send(Q.at[own_rows], Q.at[own_rows], sq.at[0, da], rq.at[mine], at(A + da, B))

    def to_sib(r, i):
        send(Q.at[rows_of(r)], Q.at[rows_of(r)], ssq.at[i], rq.at[r], sib)

    def spread(da):
        r = slot(c, B, A - da)
        rr = rows_of(r)
        if da:
            arrived(Q.at[rr], rq.at[r])
        for i, db in enumerate((1, -1)):
            send(Q.at[rr], Q.at[rr], sq.at[1 + i, da], rq.at[r], at(A, B + db))
        to_sib(r, da)

    def pass_on(da):
        for i, db in enumerate((1, -1)):
            r = slot(c, B - db, A - da)
            rr = rows_of(r)
            arrived(Q.at[rr], rq.at[r])
            if da % 2 == i:
                send(Q.at[rr], Q.at[rr], sq.at[3, da], rq.at[r], at(A, B + db))
            to_sib(r, 4 + 4 * i + da)

    def columns_on(f):
        arrived(C.at[crows(1), fcols(f)], rx.at[0, f])
        send(C.at[crows(1), fcols(f)], C.at[crows(3), fcols(f)], sx.at[2, f], rx.at[2, f], right)
        h = f + 2
        arrived(C.at[crows(2), fcols(h)], rx.at[1, h])
        send(C.at[crows(2), fcols(h)], C.at[crows(3), fcols(h)], sx.at[2, h], rx.at[2, h], left)

    for da in (0, 1, 3):
        spread(da)
    pass_on(0)
    spread(2)
    columns_on(0)
    pass_on(1)
    pass_on(3)
    columns_on(1)
    pass_on(2)
    for da in (0, 1, 3, 2):
        r = slot(c, B + 2, A - da)
        arrived(Q.at[rows_of(r)], rq.at[r])
        to_sib(r, 12 + da)
    for k in range(16):
        r = (1 - c) * 16 + k
        arrived(Q.at[rows_of(r)], rq.at[r])

    ext = jnp.transpose(Q[:, D : D + EXT].astype(F32))
    ids = ext[0:8] * 128.0 + ext[8:16]
    col_neg = lax.broadcasted_iota(jnp.int32, (NEG, 512), 0)
    col_pas = lax.broadcasted_iota(jnp.int32, (ROWS, 512), 0)
    for k, dx in enumerate((0, 3, 1, 2)):
        lin = ((y % 2) * 4 + (x + dx) % 4) * 16 + g_id
        gid = (col_neg + lin * NEG).astype(F32)
        mult = jnp.zeros((NEG, 512), F32)
        for h in range(7):
            mult = mult + (ids[h : h + 1] == gid).astype(F32)
        MU[k * COLS : k * COLS + NEG, :] = mult
        pid = (col_pas + lin * ROWS).astype(F32)
        MU[k * COLS + NEG : (k + 1) * COLS, :] = (ids[7:8] == pid).astype(F32)

    def dots(lo, hi, d0, d1):
        return lax.dot_general(
            C[lo:hi, d0:d1], Q[:, d0:d1], (((1,), (1,)), ((), ())), preferred_element_type=F32
        )

    def partial_stats(lo, hi):
        for k in range(lo // COLS, hi // COLS):
            r0, r1 = k * COLS, k * COLS + NEG
            S[r0:r1, :] = jnp.where(MU[r0:r1, :] > 0.0, S[r0:r1, :], FLOOR)
        m = jnp.max(S[lo:hi, :], 0, keepdims=True)
        tot = jnp.zeros((1, 512), F32)
        for k in range(lo // COLS, hi // COLS):
            r0, r1, r2 = k * COLS, k * COLS + NEG, (k + 1) * COLS
            tot = tot + jnp.sum(jnp.exp(S[r0:r1, :] - m) * MU[r0:r1, :], 0, keepdims=True)
            tot = tot + jnp.sum(jnp.exp(S[r1:r2, :] - m), 0, keepdims=True)
        return m, tot

    for f in (2, 3):
        arrived(C.at[crows(1), fcols(f)], rx.at[0, f])
        arrived(C.at[crows(2), fcols(f - 2)], rx.at[1, f - 2])
    S[0 : 3 * COLS, :] = INV * dots(0, 3 * COLS, 0, D)
    m_a, tot_a = partial_stats(0, 3 * COLS)
    acc = jnp.zeros((COLS, 512), F32)
    for f in (0, 2, 1, 3):
        arrived(C.at[crows(3), fcols(f)], rx.at[2, f])
        acc = acc + dots(3 * COLS, 4 * COLS, f * CH, (f + 1) * CH)
    S[3 * COLS : 4 * COLS, :] = INV * acc
    m_b, tot_b = partial_stats(3 * COLS, 4 * COLS)

    m = jnp.maximum(m_a, m_b)
    tot = tot_a * jnp.exp(m_a - m) + tot_b * jnp.exp(m_b - m)
    for j in range(4):
        st1[0, j : j + 1, :] = m[:, j * 128 : (j + 1) * 128]
        st1[0, 4 + j : 5 + j, :] = tot[:, j * 128 : (j + 1) * 128]

    def merge(buf, n):
        top = buf[0, 0:4, :]
        for i in range(1, n):
            top = jnp.maximum(top, buf[i, 0:4, :])
        total = jnp.zeros((4, 128), F32)
        for i in range(n):
            total = total + buf[i, 4:8, :] * jnp.exp(buf[i, 0:4, :] - top)
        return top, total

    for i in range(1, 8):
        dy, dc = i // 2, i % 2
        send(st1.at[0], st1.at[i], sst.at[i], rst1.at[i], dev(x, y + dy, z, (c + dc) % 2))
    for i in range(1, 8):
        arrived(st1.at[i], rst1.at[i])
    top, total = merge(st1, 8)
    st2[0, 0:4, :] = top
    st2[0, 4:8, :] = total
    for i in range(1, 4):
        send(st2.at[0], st2.at[i], sst.at[7 + i], rst2.at[i], dev(x, y, z + i, c))
    for i in range(1, 4):
        arrived(st2.at[i], rst2.at[i])
    top, total = merge(st2, 4)
    lt = top + jnp.log(total)
    log_total = jnp.concatenate([lt[j : j + 1, :] for j in range(4)], 1)

    def weights(k):
        r0, r1, r2 = k * COLS, k * COLS + NEG, (k + 1) * COLS
        hard = jnp.exp(S[r0:r1, :] - log_total).astype(BF).astype(F32) * MU[r0:r1, :]
        W[r0:r1, :] = hard.astype(BF)
        W[r1:r2, :] = (jnp.exp(S[r1:r2, :] - log_total) - MU[r1:r2, :]).astype(BF)

    def col_grad(lo, hi, f):
        return INV * jnp.dot(W[lo:hi, :], Q[:, f * CH : (f + 1) * CH], preferred_element_type=F32)

    weights(3)
    for f in (0, 2, 1, 3):
        g3[:, f * CH : (f + 1) * CH] = col_grad(3 * COLS, 4 * COLS, f).astype(BF)
        to = right if f < 2 else left
        send(g3.at[:, fcols(f)], rx2.at[:, fcols(f)], sg.at[0, f], rg2.at[f], to)
    for k in (0, 1, 2):
        weights(k)

    def query_grad(core, f):
        w = W[:, pl.ds(pl.multiple_of(core * 256, 256), 256)]
        return INV * lax.dot_general(
            w, C[:, f * CH : (f + 1) * CH], (((0,), (0,)), ((), ())), preferred_element_type=F32
        )

    def half(i):
        return pl.ds(32 * i, 32)

    def group(b, i):
        return rows_of(slot(0, b, 2 * i), 32)

    for f in range(NF):
        sibs[:, f * CH : (f + 1) * CH] = query_grad(1 - c, f).astype(BF)
        send(sibs.at[:, fcols(f)], rsib.at[:, fcols(f)], ssib.at[f], rsibs.at[f], sib)
    for f in range(NF):
        cs = slice(f * CH, (f + 1) * CH)
        g12[:, cs] = col_grad(COLS, 3 * COLS, f)
        if f < 2:
            gsend[0:COLS, cs] = g12[0:COLS, cs].astype(BF)
            send(gsend.at[pl.ds(0, COLS), fcols(f)], rf2.at[:, fcols(f)], sg.at[1, f], rgf2.at[f], left)
        else:
            gsend[COLS:, cs] = g12[COLS:, cs].astype(BF)
            send(gsend.at[pl.ds(COLS, COLS), fcols(f)], rf1.at[:, fcols(f)], sg.at[1, f], rgf1.at[f], right)
    for f in range(NF):
        ownq[:, f * CH : (f + 1) * CH] = query_grad(c, f)
    for f in range(NF):
        cs = slice(f * CH, (f + 1) * CH)
        arrived(rsib.at[:, fcols(f)], rsibs.at[f])
        G[:, cs] = (ownq[:, cs] + rsib[:, cs].astype(F32)).astype(BF)
        for i, db in enumerate((1, -1)):
            h, o = half(i), half(1 - i)
            src = G.at[group(B + 2, i), fcols(f)]
            send(src, rB2.at[h, fcols(f)], sB.at[0, i, f], rB2s.at[i, f], at(A, B + db))
            src = G.at[group(B + db, 1 - i), fcols(f)]
            send(src, rB.at[i, o, fcols(f)], sB.at[1, i, f], rBs.at[i, 1 - i, f], at(A, B + db))
    for f in range(NF):
        cs = slice(f * CH, (f + 1) * CH)
        for i, db in enumerate((1, -1)):
            h = half(i)
            arrived(rB2.at[h, fcols(f)], rB2s.at[i, f])
            t = G[group(B + db, i), cs].astype(F32) + rB2[h, cs].astype(F32)
            gB[h, cs] = t.astype(BF)
            send(gB.at[h, fcols(f)], rB.at[i, h, fcols(f)], sB.at[2, i, f], rBs.at[i, i, f], at(A, B + db))
    for f in (0, 2, 1, 3):
        cs = slice(f * CH, (f + 1) * CH)
        arrived(rx2.at[:, fcols(f)], rg2.at[f])
        if f < 2:
            gsend[COLS:, cs] = (g12[COLS:, cs] + rx2[:, cs].astype(F32)).astype(BF)
            send(gsend.at[pl.ds(COLS, COLS), fcols(f)], rf1.at[:, fcols(f)], sg.at[2, f], rgf1.at[f], right)
        else:
            gsend[0:COLS, cs] = (g12[0:COLS, cs] + rx2[:, cs].astype(F32)).astype(BF)
            send(gsend.at[pl.ds(0, COLS), fcols(f)], rf2.at[:, fcols(f)], sg.at[2, f], rgf2.at[f], left)
    for f in range(NF):
        g0[:, f * CH : (f + 1) * CH] = col_grad(0, COLS, f)
    for f in range(NF):
        cs = slice(f * CH, (f + 1) * CH)
        t = G[rows_of(slot(0, B, 0), 64), cs].astype(F32)
        for i in range(2):
            for j in range(2):
                arrived(rB.at[i, half(j), fcols(f)], rBs.at[i, j, f])
            t = t + rB[i, :, cs].astype(F32)
        T[:, cs] = t.astype(BF)
        for da in (2, 1, 3):
            src = T.at[rows_of(slot(0, 0, A + da)), fcols(f)]
            send(src, rA.at[da, :, fcols(f)], sA.at[da, f], rAs.at[da, f], at(A + da, B))
    for f in range(NF):
        cs = slice(f * CH, (f + 1) * CH)
        t = T[rows_of(A), cs].astype(F32)
        for da in (1, 2, 3):
            arrived(rA.at[da, :, fcols(f)], rAs.at[da, f])
            t = t + rA[da, :, cs].astype(F32)
        out[0:ROWS, cs] = t.astype(BF)
    for f in (2, 0, 3, 1):
        cs = slice(f * CH, (f + 1) * CH)
        arrived(rf1.at[:, fcols(f)], rgf1.at[f])
        arrived(rf2.at[:, fcols(f)], rgf2.at[f])
        t = g0[:, cs] + rf1[:, cs].astype(F32) + rf2[:, cs].astype(F32)
        out[2 * ROWS :, cs] = t[0:NEG].astype(BF)
        out[ROWS : 2 * ROWS, cs] = t[NEG:COLS].astype(BF)
    for cp in sent:
        cp.wait_send()


def on_device(queries, document_vectors, negatives, positives, neg_ids):
    dma = pltpu.SemaphoreType.DMA
    vm = pltpu.VMEM
    hbm = [
        pltpu.with_memory_space_constraint(a, pltpu.HBM)
        for a in (queries, document_vectors, negatives, positives.reshape(1, ROWS), neg_ids.T)
    ]
    out = pl.pallas_call(
        kernel,
        out_shape=pltpu.VMEM((2 * ROWS + NEG, D), BF),
        in_specs=[pl.BlockSpec(memory_space=pltpu.HBM)] * 5,
        scratch_shapes=[
            vm((1, ROWS), jnp.int32),
            vm((7, ROWS), jnp.int32),
            vm((128, 128), F32),
            vm((512, D + EXT), BF),
            vm((4 * COLS, D), BF),
            vm((4 * COLS, 512), F32),
            vm((4 * COLS, 512), BF),
            vm((4 * COLS, 512), F32),
            vm((256, D), BF),
            vm((256, D), F32),
            vm((256, D), BF),
            vm((256, D), BF),
            vm((64, D), BF),
            vm((64, D), BF),
            vm((2, 64, D), BF),
            vm((64, D), BF),
            vm((4, ROWS, D), BF),
            vm((COLS, D), BF),
            vm((2 * COLS, D), F32),
            vm((2 * COLS, D), BF),
            vm((COLS, D), F32),
            vm((COLS, D), BF),
            vm((COLS, D), BF),
            vm((COLS, D), BF),
            vm((8, 8, 128), F32),
            vm((4, 8, 128), F32),
            dma((5,)),
            dma((3, NF)),
            dma((3, NF)),
            dma((4, 4)),
            dma((16,)),
            dma((32,)),
            dma((11,)),
            dma((8,)),
            dma((4,)),
            dma((3, NF)),
            dma((NF,)),
            dma((NF,)),
            dma((NF,)),
            dma((NF,)),
            dma((NF,)),
            dma((3, 2, NF)),
            dma((2, NF)),
            dma((2, 2, NF)),
            dma((4, NF)),
            dma((4, NF)),
        ],
        compiler_params=pltpu.CompilerParams(
            collective_id=0, has_side_effects=True, vmem_limit_bytes=44 * 2**20
        ),
    )(*hbm)
    return out[0:ROWS], out[ROWS : 2 * ROWS], out[2 * ROWS :]


def solution(mesh):
    rows = P(("blk", "grp"), None)
    return jax.shard_map(
        on_device,
        mesh=mesh,
        in_specs=(rows, rows, rows, P(("blk", "grp")), rows),
        out_specs=(rows, rows, rows),
        check_vma=False,
    )
```

```python
import jax
import jax.numpy as jnp
from jax import lax
from jax.experimental import pallas as pl
from jax.experimental.pallas import tpu as pltpu
from jax.sharding import PartitionSpec as P

MESH = pl.DeviceIdType.MESH
BF = jnp.bfloat16
F32 = jnp.float32
INV = 50.0
D = 4096
EXT = 128
NEG = 64
ROWS = 16
COLS = NEG + ROWS
CH = 1024
NF = D // CH
FLOOR = -1e30


def kernel(
    q_in, p_in, n_in, pos_in, ids_in, out,
    PO, ID, E, Q, C, S, W, MU, sibs, ownq, rsib, G, rB2, gB, rB, T, rA, g3, g12, gsend, g0, rx2, rf1, rf2, st1,
    lsem, sx, rx, sq, ssq, rq, sst, rst1, sg, rg2, rgf1, rgf2, ssib, rsibs, sB, rB2s, rBs, sA, rAs,
):
    b_id = lax.axis_index("blk")
    g_id = lax.axis_index("grp")
    x = b_id % 4
    y = (g_id // 8) * 2 + b_id // 4
    z = (g_id // 2) % 4
    c = g_id % 2

    def dev(xx, yy, zz, cc):
        xx, yy, zz = (xx + 4) % 4, (yy + 4) % 4, (zz + 4) % 4
        return {"blk": (yy % 2) * 4 + xx, "grp": ((yy // 2) * 4 + zz) * 2 + cc}

    right, left, sib = dev(x + 1, y, z, c), dev(x - 1, y, z, c), dev(x, y, z, 1 - c)
    A = z + c * (y - z)
    B = y + c * (z - y)

    def at(a, b):
        a, b = (a + 4) % 4, (b + 4) % 4
        return dev(x, b + c * (a - b), a + c * (b - a), c)

    def slot(cc, b, a):
        return cc * 16 + ((b + 4) % 4) * 4 + (a + 4) % 4

    def rows_of(s, count=ROWS):
        return pl.ds(pl.multiple_of(s * ROWS, ROWS), count)

    sent = []

    def send(src, dst, ss, rs, to):
        cp = pltpu.make_async_remote_copy(
            src_ref=src, dst_ref=dst, send_sem=ss, recv_sem=rs, device_id=to, device_id_type=MESH
        )
        cp.start()
        sent.append(cp)

    def arrived(dst, rs):
        pltpu.make_async_remote_copy(
            src_ref=dst, dst_ref=dst, send_sem=lsem.at[0], recv_sem=rs, device_id=sib, device_id_type=MESH
        ).wait_recv()

    mine = slot(c, B, A)
    own_rows = rows_of(mine)
    local = [
        pltpu.make_async_copy(n_in, C.at[pl.ds(0, NEG)], lsem.at[0]),
        pltpu.make_async_copy(p_in, C.at[pl.ds(NEG, ROWS)], lsem.at[1]),
        pltpu.make_async_copy(q_in, Q.at[own_rows, pl.ds(0, D)], lsem.at[2]),
        pltpu.make_async_copy(pos_in, PO, lsem.at[3]),
        pltpu.make_async_copy(ids_in, ID, lsem.at[4]),
    ]
    for cp in local:
        cp.start()
    barrier = pltpu.get_barrier_semaphore()
    greet = [dev(x, y + dy, z, cc) for dy in (2, 1, 3) for cc in (0, 1)]
    greet += [dev(x, y, z + dz, c) for dz in (2, 1, 3)]
    greet += [right, left, sib]
    for to in greet:
        pl.semaphore_signal(barrier, inc=1, device_id=to, device_id_type=MESH)
    E[...] = jnp.zeros((128, 128), F32)
    for cp in local:
        cp.wait()
    for r, part in ((0, ID[...]), (7, PO[...])):
        n = part.shape[0]
        E[r : r + n, 0:ROWS] = (part // 128).astype(F32)
        E[8 + r : 8 + r + n, 0:ROWS] = (part % 128).astype(F32)
    Q[own_rows, D : D + EXT] = jnp.transpose(E[...])[0:ROWS].astype(BF)
    pl.semaphore_wait(barrier, len(greet))

    def fcols(f):
        return pl.ds(f * CH, CH)

    def crows(k):
        return pl.ds(k * COLS, COLS)

    for i in range(NF):
        f, h = i, (i + 2) % 4
        send(C.at[crows(0), fcols(f)], C.at[crows(1), fcols(f)], sx.at[0, f], rx.at[0, f], right)
        send(C.at[crows(0), fcols(h)], C.at[crows(2), fcols(h)], sx.at[1, h], rx.at[1, h], left)
    for da in (1, 3, 2):
        send(Q.at[own_rows], Q.at[own_rows], sq.at[0, da], rq.at[mine], at(A + da, B))

    def to_sib(r, i):
        send(Q.at[rows_of(r)], Q.at[rows_of(r)], ssq.at[i], rq.at[r], sib)

    def spread(da):
        r = slot(c, B, A - da)
        rr = rows_of(r)
        if da:
            arrived(Q.at[rr], rq.at[r])
        for i, db in enumerate((1, -1)):
            send(Q.at[rr], Q.at[rr], sq.at[1 + i, da], rq.at[r], at(A, B + db))
        to_sib(r, da)

    def pass_on(da):
        for i, db in enumerate((1, -1)):
            r = slot(c, B - db, A - da)
            rr = rows_of(r)
            arrived(Q.at[rr], rq.at[r])
            if da % 2 == i:
                send(Q.at[rr], Q.at[rr], sq.at[3, da], rq.at[r], at(A, B + db))
            to_sib(r, 4 + 4 * i + da)

    def columns_on(f):
        arrived(C.at[crows(1), fcols(f)], rx.at[0, f])
        send(C.at[crows(1), fcols(f)], C.at[crows(3), fcols(f)], sx.at[2, f], rx.at[2, f], right)
        h = f + 2
        arrived(C.at[crows(2), fcols(h)], rx.at[1, h])
        send(C.at[crows(2), fcols(h)], C.at[crows(3), fcols(h)], sx.at[2, h], rx.at[2, h], left)

    for da in (0, 1, 3):
        spread(da)
    pass_on(0)
    spread(2)
    columns_on(0)
    pass_on(1)
    pass_on(3)
    columns_on(1)
    pass_on(2)
    for da in (0, 1, 3, 2):
        r = slot(c, B + 2, A - da)
        arrived(Q.at[rows_of(r)], rq.at[r])
        to_sib(r, 12 + da)
    for k in range(16):
        r = (1 - c) * 16 + k
        arrived(Q.at[rows_of(r)], rq.at[r])

    ext = jnp.transpose(Q[:, D : D + EXT].astype(F32))
    ids = ext[0:8] * 128.0 + ext[8:16]
    col_neg = lax.broadcasted_iota(jnp.int32, (NEG, 512), 0)
    col_pas = lax.broadcasted_iota(jnp.int32, (ROWS, 512), 0)
    for k, dx in enumerate((0, 3, 1, 2)):
        lin = ((y % 2) * 4 + (x + dx) % 4) * 16 + g_id
        gid = (col_neg + lin * NEG).astype(F32)
        mult = jnp.zeros((NEG, 512), F32)
        for h in range(7):
            mult = mult + (ids[h : h + 1] == gid).astype(F32)
        MU[k * COLS : k * COLS + NEG, :] = mult
        pid = (col_pas + lin * ROWS).astype(F32)
        MU[k * COLS + NEG : (k + 1) * COLS, :] = (ids[7:8] == pid).astype(F32)

    def dots(lo, hi, d0, d1):
        return lax.dot_general(
            C[lo:hi, d0:d1], Q[:, d0:d1], (((1,), (1,)), ((), ())), preferred_element_type=F32
        )

    def partial_stats(lo, hi):
        for k in range(lo // COLS, hi // COLS):
            r0, r1 = k * COLS, k * COLS + NEG
            S[r0:r1, :] = jnp.where(MU[r0:r1, :] > 0.0, S[r0:r1, :], FLOOR)
        m = jnp.max(S[lo:hi, :], 0, keepdims=True)
        tot = jnp.zeros((1, 512), F32)
        for k in range(lo // COLS, hi // COLS):
            r0, r1, r2 = k * COLS, k * COLS + NEG, (k + 1) * COLS
            tot = tot + jnp.sum(jnp.exp(S[r0:r1, :] - m) * MU[r0:r1, :], 0, keepdims=True)
            tot = tot + jnp.sum(jnp.exp(S[r1:r2, :] - m), 0, keepdims=True)
        return m, tot

    for f in (2, 3):
        arrived(C.at[crows(1), fcols(f)], rx.at[0, f])
        arrived(C.at[crows(2), fcols(f - 2)], rx.at[1, f - 2])
    S[0 : 3 * COLS, :] = INV * dots(0, 3 * COLS, 0, D)
    m_a, tot_a = partial_stats(0, 3 * COLS)
    acc = jnp.zeros((COLS, 512), F32)
    for f in (0, 2, 1, 3):
        arrived(C.at[crows(3), fcols(f)], rx.at[2, f])
        acc = acc + dots(3 * COLS, 4 * COLS, f * CH, (f + 1) * CH)
    S[3 * COLS : 4 * COLS, :] = INV * acc
    m_b, tot_b = partial_stats(3 * COLS, 4 * COLS)

    m = jnp.maximum(m_a, m_b)
    tot = tot_a * jnp.exp(m_a - m) + tot_b * jnp.exp(m_b - m)
    for j in range(4):
        st1[0, j : j + 1, :] = m[:, j * 128 : (j + 1) * 128]
        st1[0, 4 + j : 5 + j, :] = tot[:, j * 128 : (j + 1) * 128]

    def merge(buf, n):
        top = buf[0, 0:4, :]
        for i in range(1, n):
            top = jnp.maximum(top, buf[i, 0:4, :])
        total = jnp.zeros((4, 128), F32)
        for i in range(n):
            total = total + buf[i, 4:8, :] * jnp.exp(buf[i, 0:4, :] - top)
        return top, total

    for i in (*range(16, 24), *range(8, 16), *range(24, 32), *range(1, 8)):
        dy, dz, dc = i // 8, i // 2 % 4, i % 2
        send(st1.at[0], st1.at[i], sst.at[i], rst1.at[i], dev(x, y + dy, z + dz, (c + dc) % 2))
    for i in range(1, 32):
        arrived(st1.at[i], rst1.at[i])
    top, total = merge(st1, 32)
    lt = top + jnp.log(total)
    log_total = jnp.concatenate([lt[j : j + 1, :] for j in range(4)], 1)

    def weights(k):
        r0, r1, r2 = k * COLS, k * COLS + NEG, (k + 1) * COLS
        hard = jnp.exp(S[r0:r1, :] - log_total).astype(BF).astype(F32) * MU[r0:r1, :]
        W[r0:r1, :] = hard.astype(BF)
        W[r1:r2, :] = (jnp.exp(S[r1:r2, :] - log_total) - MU[r1:r2, :]).astype(BF)

    def col_grad(lo, hi, f):
        return INV * jnp.dot(W[lo:hi, :], Q[:, f * CH : (f + 1) * CH], preferred_element_type=F32)

    weights(3)
    for f in (0, 2, 1, 3):
        g3[:, f * CH : (f + 1) * CH] = col_grad(3 * COLS, 4 * COLS, f).astype(BF)
        to = right if f < 2 else left
        send(g3.at[:, fcols(f)], rx2.at[:, fcols(f)], sg.at[0, f], rg2.at[f], to)
    for k in (0, 1, 2):
        weights(k)

    def query_grad(core, f):
        w = W[:, pl.ds(pl.multiple_of(core * 256, 256), 256)]
        return INV * lax.dot_general(
            w, C[:, f * CH : (f + 1) * CH], (((0,), (0,)), ((), ())), preferred_element_type=F32
        )

    def half(i):
        return pl.ds(32 * i, 32)

    def group(b, i):
        return rows_of(slot(0, b, 2 * i), 32)

    for f in range(NF):
        sibs[:, f * CH : (f + 1) * CH] = query_grad(1 - c, f).astype(BF)
        send(sibs.at[:, fcols(f)], rsib.at[:, fcols(f)], ssib.at[f], rsibs.at[f], sib)
    for f in range(NF):
        cs = slice(f * CH, (f + 1) * CH)
        g12[:, cs] = col_grad(COLS, 3 * COLS, f)
        if f < 2:
            gsend[0:COLS, cs] = g12[0:COLS, cs].astype(BF)
            send(gsend.at[pl.ds(0, COLS), fcols(f)], rf2.at[:, fcols(f)], sg.at[1, f], rgf2.at[f], left)
        else:
            gsend[COLS:, cs] = g12[COLS:, cs].astype(BF)
            send(gsend.at[pl.ds(COLS, COLS), fcols(f)], rf1.at[:, fcols(f)], sg.at[1, f], rgf1.at[f], right)
    for f in range(NF):
        ownq[:, f * CH : (f + 1) * CH] = query_grad(c, f)
    for f in range(NF):
        cs = slice(f * CH, (f + 1) * CH)
        arrived(rsib.at[:, fcols(f)], rsibs.at[f])
        G[:, cs] = (ownq[:, cs] + rsib[:, cs].astype(F32)).astype(BF)
        for i, db in enumerate((1, -1)):
            h, o = half(i), half(1 - i)
            src = G.at[group(B + 2, i), fcols(f)]
            send(src, rB2.at[h, fcols(f)], sB.at[0, i, f], rB2s.at[i, f], at(A, B + db))
            src = G.at[group(B + db, 1 - i), fcols(f)]
            send(src, rB.at[i, o, fcols(f)], sB.at[1, i, f], rBs.at[i, 1 - i, f], at(A, B + db))
    for f in range(NF):
        cs = slice(f * CH, (f + 1) * CH)
        for i, db in enumerate((1, -1)):
            h = half(i)
            arrived(rB2.at[h, fcols(f)], rB2s.at[i, f])
            t = G[group(B + db, i), cs].astype(F32) + rB2[h, cs].astype(F32)
            gB[h, cs] = t.astype(BF)
            send(gB.at[h, fcols(f)], rB.at[i, h, fcols(f)], sB.at[2, i, f], rBs.at[i, i, f], at(A, B + db))
    for f in (0, 2, 1, 3):
        cs = slice(f * CH, (f + 1) * CH)
        arrived(rx2.at[:, fcols(f)], rg2.at[f])
        if f < 2:
            gsend[COLS:, cs] = (g12[COLS:, cs] + rx2[:, cs].astype(F32)).astype(BF)
            send(gsend.at[pl.ds(COLS, COLS), fcols(f)], rf1.at[:, fcols(f)], sg.at[2, f], rgf1.at[f], right)
        else:
            gsend[0:COLS, cs] = (g12[0:COLS, cs] + rx2[:, cs].astype(F32)).astype(BF)
            send(gsend.at[pl.ds(0, COLS), fcols(f)], rf2.at[:, fcols(f)], sg.at[2, f], rgf2.at[f], left)
    for f in range(NF):
        g0[:, f * CH : (f + 1) * CH] = col_grad(0, COLS, f)
    for f in range(NF):
        cs = slice(f * CH, (f + 1) * CH)
        t = G[rows_of(slot(0, B, 0), 64), cs].astype(F32)
        for i in range(2):
            for j in range(2):
                arrived(rB.at[i, half(j), fcols(f)], rBs.at[i, j, f])
            t = t + rB[i, :, cs].astype(F32)
        T[:, cs] = t.astype(BF)
        for da in (2, 1, 3):
            src = T.at[rows_of(slot(0, 0, A + da)), fcols(f)]
            send(src, rA.at[da, :, fcols(f)], sA.at[da, f], rAs.at[da, f], at(A + da, B))
    for f in range(NF):
        cs = slice(f * CH, (f + 1) * CH)
        t = T[rows_of(A), cs].astype(F32)
        for da in (1, 2, 3):
            arrived(rA.at[da, :, fcols(f)], rAs.at[da, f])
            t = t + rA[da, :, cs].astype(F32)
        out[0:ROWS, cs] = t.astype(BF)
    for f in (2, 0, 3, 1):
        cs = slice(f * CH, (f + 1) * CH)
        arrived(rf1.at[:, fcols(f)], rgf1.at[f])
        arrived(rf2.at[:, fcols(f)], rgf2.at[f])
        t = g0[:, cs] + rf1[:, cs].astype(F32) + rf2[:, cs].astype(F32)
        out[2 * ROWS :, cs] = t[0:NEG].astype(BF)
        out[ROWS : 2 * ROWS, cs] = t[NEG:COLS].astype(BF)
    for cp in sent:
        cp.wait_send()


def on_device(queries, document_vectors, negatives, positives, neg_ids):
    dma = pltpu.SemaphoreType.DMA
    vm = pltpu.VMEM
    hbm = [
        pltpu.with_memory_space_constraint(a, pltpu.HBM)
        for a in (queries, document_vectors, negatives, positives.reshape(1, ROWS), neg_ids.T)
    ]
    out = pl.pallas_call(
        kernel,
        out_shape=pltpu.VMEM((2 * ROWS + NEG, D), BF),
        in_specs=[pl.BlockSpec(memory_space=pltpu.HBM)] * 5,
        scratch_shapes=[
            vm((1, ROWS), jnp.int32),
            vm((7, ROWS), jnp.int32),
            vm((128, 128), F32),
            vm((512, D + EXT), BF),
            vm((4 * COLS, D), BF),
            vm((4 * COLS, 512), F32),
            vm((4 * COLS, 512), BF),
            vm((4 * COLS, 512), F32),
            vm((256, D), BF),
            vm((256, D), F32),
            vm((256, D), BF),
            vm((256, D), BF),
            vm((64, D), BF),
            vm((64, D), BF),
            vm((2, 64, D), BF),
            vm((64, D), BF),
            vm((4, ROWS, D), BF),
            vm((COLS, D), BF),
            vm((2 * COLS, D), F32),
            vm((2 * COLS, D), BF),
            vm((COLS, D), F32),
            vm((COLS, D), BF),
            vm((COLS, D), BF),
            vm((COLS, D), BF),
            vm((32, 8, 128), F32),
            dma((5,)),
            dma((3, NF)),
            dma((3, NF)),
            dma((4, 4)),
            dma((16,)),
            dma((32,)),
            dma((32,)),
            dma((32,)),
            dma((3, NF)),
            dma((NF,)),
            dma((NF,)),
            dma((NF,)),
            dma((NF,)),
            dma((NF,)),
            dma((3, 2, NF)),
            dma((2, NF)),
            dma((2, 2, NF)),
            dma((4, NF)),
            dma((4, NF)),
        ],
        compiler_params=pltpu.CompilerParams(
            collective_id=0, has_side_effects=True, vmem_limit_bytes=44 * 2**20
        ),
    )(*hbm)
    return out[0:ROWS], out[ROWS : 2 * ROWS], out[2 * ROWS :]


def solution(mesh):
    rows = P(("blk", "grp"), None)
    return jax.shard_map(
        on_device,
        mesh=mesh,
        in_specs=(rows, rows, rows, P(("blk", "grp")), rows),
        out_specs=(rows, rows, rows),
        check_vma=False,
    )
```

```python
import jax
import jax.numpy as jnp
from jax import lax
from jax.experimental import pallas as pl
from jax.experimental.pallas import tpu as pltpu
from jax.sharding import PartitionSpec as P

MESH = pl.DeviceIdType.MESH
BF = jnp.bfloat16
F32 = jnp.float32
INV = 50.0
D = 4096
EXT = 128
NEG = 64
ROWS = 16
COLS = NEG + ROWS
CH = 1024
NF = D // CH
FLOOR = -1e30


def kernel(
    q_in, p_in, n_in, pos_in, ids_in, out,
    PO, ID, E, Q, C, S, W, MU, sibs, ownq, rsib, G, rB2, gB, rB, T, rA, g3, g12, gsend, g0, rx2, rf1, rf2, st1, MT,
    lsem, sx, rx, sq, ssq, rq, sst, rst1, sg, rg2, rgf1, rgf2, ssib, rsibs, sB, rB2s, rBs, sA, rAs,
):
    b_id = lax.axis_index("blk")
    g_id = lax.axis_index("grp")
    x = b_id % 4
    y = (g_id // 8) * 2 + b_id // 4
    z = (g_id // 2) % 4
    c = g_id % 2

    def dev(xx, yy, zz, cc):
        xx, yy, zz = (xx + 4) % 4, (yy + 4) % 4, (zz + 4) % 4
        return {"blk": (yy % 2) * 4 + xx, "grp": ((yy // 2) * 4 + zz) * 2 + cc}

    right, left, sib = dev(x + 1, y, z, c), dev(x - 1, y, z, c), dev(x, y, z, 1 - c)
    A = z + c * (y - z)
    B = y + c * (z - y)

    def at(a, b):
        a, b = (a + 4) % 4, (b + 4) % 4
        return dev(x, b + c * (a - b), a + c * (b - a), c)

    def slot(cc, b, a):
        return cc * 16 + ((b + 4) % 4) * 4 + (a + 4) % 4

    def rows_of(s, count=ROWS):
        return pl.ds(pl.multiple_of(s * ROWS, ROWS), count)

    sent = []

    def send(src, dst, ss, rs, to):
        cp = pltpu.make_async_remote_copy(
            src_ref=src, dst_ref=dst, send_sem=ss, recv_sem=rs, device_id=to, device_id_type=MESH
        )
        cp.start()
        sent.append(cp)

    def flush():
        for cp in sent:
            cp.wait_send()
        sent.clear()

    def arrived(dst, rs):
        pltpu.make_async_remote_copy(
            src_ref=dst, dst_ref=dst, send_sem=lsem.at[0], recv_sem=rs, device_id=sib, device_id_type=MESH
        ).wait_recv()

    mine = slot(c, B, A)
    own_rows = rows_of(mine)
    local = [
        pltpu.make_async_copy(n_in, C.at[pl.ds(0, NEG)], lsem.at[0]),
        pltpu.make_async_copy(p_in, C.at[pl.ds(NEG, ROWS)], lsem.at[1]),
        pltpu.make_async_copy(q_in, Q.at[own_rows, pl.ds(0, D)], lsem.at[2]),
        pltpu.make_async_copy(pos_in, PO, lsem.at[3]),
        pltpu.make_async_copy(ids_in, ID, lsem.at[4]),
    ]
    for cp in local:
        cp.start()
    barrier = pltpu.get_barrier_semaphore()
    greet = [at(A + 2, B), at(A, B + 2), at(A + 1, B), at(A - 1, B), at(A, B + 1), at(A, B - 1), right, left, sib]
    for to in greet:
        pl.semaphore_signal(barrier, inc=1, device_id=to, device_id_type=MESH)
    E[...] = jnp.zeros((128, 128), F32)
    for cp in local:
        cp.wait()
    for r, part in ((0, ID[...]), (7, PO[...])):
        n = part.shape[0]
        E[r : r + n, 0:ROWS] = (part // 128).astype(F32)
        E[8 + r : 8 + r + n, 0:ROWS] = (part % 128).astype(F32)
    Q[own_rows, D : D + EXT] = jnp.transpose(E[...])[0:ROWS].astype(BF)
    pl.semaphore_wait(barrier, len(greet))

    def fcols(f):
        return pl.ds(f * CH, CH)

    def crows(k):
        return pl.ds(k * COLS, COLS)

    for i in range(NF):
        f, h = i, (i + 2) % 4
        send(C.at[crows(0), fcols(f)], C.at[crows(1), fcols(f)], sx.at[0, f], rx.at[0, f], right)
        send(C.at[crows(0), fcols(h)], C.at[crows(2), fcols(h)], sx.at[1, h], rx.at[1, h], left)
    for da in (1, 3, 2):
        send(Q.at[own_rows], Q.at[own_rows], sq.at[0, da], rq.at[mine], at(A + da, B))

    def to_sib(r, i):
        send(Q.at[rows_of(r)], Q.at[rows_of(r)], ssq.at[i], rq.at[r], sib)

    def spread(da):
        r = slot(c, B, A - da)
        rr = rows_of(r)
        if da:
            arrived(Q.at[rr], rq.at[r])
        for i, db in enumerate((1, -1)):
            send(Q.at[rr], Q.at[rr], sq.at[1 + i, da], rq.at[r], at(A, B + db))
        if da > 1:
            send(Q.at[rr], Q.at[rr], sq.at[3, da], rq.at[r], at(A, B + 2))
        to_sib(r, da)

    def pass_on(da):
        for i, db in enumerate((1, -1)):
            r = slot(c, B - db, A - da)
            rr = rows_of(r)
            arrived(Q.at[rr], rq.at[r])
            if da == i:
                send(Q.at[rr], Q.at[rr], sq.at[3, da], rq.at[r], at(A, B + db))
            to_sib(r, 4 + 4 * i + da)

    def columns_on(f):
        arrived(C.at[crows(1), fcols(f)], rx.at[0, f])
        send(C.at[crows(1), fcols(f)], C.at[crows(3), fcols(f)], sx.at[2, f], rx.at[2, f], right)
        h = f + 2
        arrived(C.at[crows(2), fcols(h)], rx.at[1, h])
        send(C.at[crows(2), fcols(h)], C.at[crows(3), fcols(h)], sx.at[2, h], rx.at[2, h], left)

    for da in (0, 1, 3):
        spread(da)
    pass_on(0)
    spread(2)
    columns_on(0)
    pass_on(1)
    pass_on(3)
    columns_on(1)
    pass_on(2)
    for da in (0, 1, 3, 2):
        r = slot(c, B + 2, A - da)
        arrived(Q.at[rows_of(r)], rq.at[r])
        to_sib(r, 12 + da)
    col_neg = lax.broadcasted_iota(jnp.int32, (NEG, 256), 0)
    col_pas = lax.broadcasted_iota(jnp.int32, (ROWS, 256), 0)

    def dots(lo, hi, rows, d0, d1):
        return INV * lax.dot_general(
            C[lo:hi, d0:d1], Q[rows, d0:d1], (((1,), (1,)), ((), ())), preferred_element_type=F32
        )

    def partial_stats(lo, hi, qs):
        for k in range(lo // COLS, hi // COLS):
            r0, r1 = k * COLS, k * COLS + NEG
            S[r0:r1, qs] = jnp.where(MU[r0:r1, qs] > 0.0, S[r0:r1, qs], FLOOR)
        m = jnp.max(S[lo:hi, qs], 0, keepdims=True)
        tot = jnp.zeros_like(m)
        for k in range(lo // COLS, hi // COLS):
            r0, r1, r2 = k * COLS, k * COLS + NEG, (k + 1) * COLS
            tot = tot + jnp.sum(jnp.exp(S[r0:r1, qs] - m) * MU[r0:r1, qs], 0, keepdims=True)
            tot = tot + jnp.sum(jnp.exp(S[r1:r2, qs] - m), 0, keepdims=True)
        return m, tot

    def half_scores(core):
        qs = pl.ds(pl.multiple_of(core * 256, 256), 256)
        ext = jnp.transpose(Q[qs, D : D + EXT].astype(F32))
        ids = ext[0:8] * 128.0 + ext[8:16]
        for k, dx in enumerate((0, 3, 1, 2)):
            lin = ((y % 2) * 4 + (x + dx) % 4) * 16 + g_id
            gid = (col_neg + lin * NEG).astype(F32)
            mult = jnp.zeros((NEG, 256), F32)
            for h in range(7):
                mult = mult + (ids[h : h + 1] == gid).astype(F32)
            MU[k * COLS : k * COLS + NEG, qs] = mult
            pid = (col_pas + lin * ROWS).astype(F32)
            MU[k * COLS + NEG : (k + 1) * COLS, qs] = (ids[7:8] == pid).astype(F32)
        S[0 : 3 * COLS, qs] = dots(0, 3 * COLS, qs, 0, D)
        m, tot = partial_stats(0, 3 * COLS, qs)
        MT[0:1, qs] = m
        MT[1:2, qs] = tot

    for f in (2, 3):
        arrived(C.at[crows(1), fcols(f)], rx.at[0, f])
        arrived(C.at[crows(2), fcols(f - 2)], rx.at[1, f - 2])
    half_scores(c)
    for k in range(16):
        r = (1 - c) * 16 + k
        arrived(Q.at[rows_of(r)], rq.at[r])
    half_scores(1 - c)
    acc = jnp.zeros((COLS, 512), F32)
    for f in (0, 2, 1, 3):
        arrived(C.at[crows(3), fcols(f)], rx.at[2, f])
        acc = acc + dots(3 * COLS, 4 * COLS, slice(0, 512), f * CH, (f + 1) * CH)
    S[3 * COLS : 4 * COLS, :] = acc
    m_b, tot_b = partial_stats(3 * COLS, 4 * COLS, slice(0, 512))
    m_a, tot_a = MT[0:1, :], MT[1:2, :]

    m = jnp.maximum(m_a, m_b)
    tot = tot_a * jnp.exp(m_a - m) + tot_b * jnp.exp(m_b - m)
    for j in range(4):
        st1[0, j : j + 1, :] = m[:, j * 128 : (j + 1) * 128]
        st1[0, 4 + j : 5 + j, :] = tot[:, j * 128 : (j + 1) * 128]

    def merge(buf, n):
        top = buf[0, 0:4, :]
        for i in range(1, n):
            top = jnp.maximum(top, buf[i, 0:4, :])
        total = jnp.zeros((4, 128), F32)
        for i in range(n):
            total = total + buf[i, 4:8, :] * jnp.exp(buf[i, 0:4, :] - top)
        return top, total

    earlier = len(sent)
    for i in (*range(16, 24), *range(8, 16), *range(24, 32), *range(1, 8)):
        dy, dz, dc = i // 8, i // 2 % 4, i % 2
        send(st1.at[0], st1.at[i], sst, rst1, dev(x, y + dy, z + dz, (c + dc) % 2))
    del sent[earlier:]
    flush()
    others = st1.at[pl.ds(1, 31)]
    arrived(others, rst1)
    top, total = merge(st1, 32)
    lt = top + jnp.log(total)
    log_total = jnp.concatenate([lt[j : j + 1, :] for j in range(4)], 1)

    def weights(k):
        r0, r1, r2 = k * COLS, k * COLS + NEG, (k + 1) * COLS
        hard = jnp.exp(S[r0:r1, :] - log_total).astype(BF).astype(F32) * MU[r0:r1, :]
        W[r0:r1, :] = hard.astype(BF)
        W[r1:r2, :] = (jnp.exp(S[r1:r2, :] - log_total) - MU[r1:r2, :]).astype(BF)

    def col_grad(lo, hi, f):
        return INV * jnp.dot(W[lo:hi, :], Q[:, f * CH : (f + 1) * CH], preferred_element_type=F32)

    weights(3)
    for f in (0, 2, 1, 3):
        g3[:, f * CH : (f + 1) * CH] = col_grad(3 * COLS, 4 * COLS, f).astype(BF)
        to = right if f < 2 else left
        send(g3.at[:, fcols(f)], rx2.at[:, fcols(f)], sg.at[0, f], rg2.at[f], to)
    for k in (0, 1, 2):
        weights(k)

    def query_grad(core, f):
        w = W[:, pl.ds(pl.multiple_of(core * 256, 256), 256)]
        return INV * lax.dot_general(
            w, C[:, f * CH : (f + 1) * CH], (((0,), (0,)), ((), ())), preferred_element_type=F32
        )

    def half(i):
        return pl.ds(32 * i, 32)

    def group(b, i):
        return rows_of(slot(0, b, 2 * i), 32)

    for f in range(NF):
        sibs[:, f * CH : (f + 1) * CH] = query_grad(1 - c, f).astype(BF)
        send(sibs.at[:, fcols(f)], rsib.at[:, fcols(f)], ssib.at[f], rsibs.at[f], sib)
    for f in range(NF):
        cs = slice(f * CH, (f + 1) * CH)
        g12[:, cs] = col_grad(COLS, 3 * COLS, f)
        if f < 2:
            gsend[0:COLS, cs] = g12[0:COLS, cs].astype(BF)
            send(gsend.at[pl.ds(0, COLS), fcols(f)], rf2.at[:, fcols(f)], sg.at[1, f], rgf2.at[f], left)
        else:
            gsend[COLS:, cs] = g12[COLS:, cs].astype(BF)
            send(gsend.at[pl.ds(COLS, COLS), fcols(f)], rf1.at[:, fcols(f)], sg.at[1, f], rgf1.at[f], right)
    for f in range(NF):
        ownq[:, f * CH : (f + 1) * CH] = query_grad(c, f)
    for f in range(NF):
        cs = slice(f * CH, (f + 1) * CH)
        arrived(rsib.at[:, fcols(f)], rsibs.at[f])
        G[:, cs] = (ownq[:, cs] + rsib[:, cs].astype(F32)).astype(BF)
        for i, db in enumerate((1, -1)):
            h, o = half(i), half(1 - i)
            src = G.at[group(B + 2, i), fcols(f)]
            send(src, rB2.at[h, fcols(f)], sB.at[0, i, f], rB2s.at[i, f], at(A, B + db))
            src = G.at[group(B + db, 1 - i), fcols(f)]
            send(src, rB.at[i, o, fcols(f)], sB.at[1, i, f], rBs.at[i, 1 - i, f], at(A, B + db))
    for f in range(NF):
        cs = slice(f * CH, (f + 1) * CH)
        for i, db in enumerate((1, -1)):
            h = half(i)
            arrived(rB2.at[h, fcols(f)], rB2s.at[i, f])
            t = G[group(B + db, i), cs].astype(F32) + rB2[h, cs].astype(F32)
            gB[h, cs] = t.astype(BF)
            send(gB.at[h, fcols(f)], rB.at[i, h, fcols(f)], sB.at[2, i, f], rBs.at[i, i, f], at(A, B + db))
    for f in (0, 2, 1, 3):
        cs = slice(f * CH, (f + 1) * CH)
        arrived(rx2.at[:, fcols(f)], rg2.at[f])
        if f < 2:
            gsend[COLS:, cs] = (g12[COLS:, cs] + rx2[:, cs].astype(F32)).astype(BF)
            send(gsend.at[pl.ds(COLS, COLS), fcols(f)], rf1.at[:, fcols(f)], sg.at[2, f], rgf1.at[f], right)
        else:
            gsend[0:COLS, cs] = (g12[0:COLS, cs] + rx2[:, cs].astype(F32)).astype(BF)
            send(gsend.at[pl.ds(0, COLS), fcols(f)], rf2.at[:, fcols(f)], sg.at[2, f], rgf2.at[f], left)
    for f in range(NF):
        g0[:, f * CH : (f + 1) * CH] = col_grad(0, COLS, f)
    for f in range(NF):
        cs = slice(f * CH, (f + 1) * CH)
        t = G[rows_of(slot(0, B, 0), 64), cs].astype(F32)
        for i in range(2):
            for j in range(2):
                arrived(rB.at[i, half(j), fcols(f)], rBs.at[i, j, f])
            t = t + rB[i, :, cs].astype(F32)
        T[:, cs] = t.astype(BF)
        for da in (2, 1, 3):
            src = T.at[rows_of(slot(0, 0, A + da)), fcols(f)]
            send(src, rA.at[da, :, fcols(f)], sA.at[da, f], rAs.at[da, f], at(A + da, B))
    flush()
    for f in range(NF):
        cs = slice(f * CH, (f + 1) * CH)
        t = T[rows_of(A), cs].astype(F32)
        for da in (1, 2, 3):
            arrived(rA.at[da, :, fcols(f)], rAs.at[da, f])
            t = t + rA[da, :, cs].astype(F32)
        out[0:ROWS, cs] = t.astype(BF)
    for f in (2, 0, 3, 1):
        cs = slice(f * CH, (f + 1) * CH)
        arrived(rf1.at[:, fcols(f)], rgf1.at[f])
        arrived(rf2.at[:, fcols(f)], rgf2.at[f])
        t = g0[:, cs] + rf1[:, cs].astype(F32) + rf2[:, cs].astype(F32)
        out[2 * ROWS :, cs] = t[0:NEG].astype(BF)
        out[ROWS : 2 * ROWS, cs] = t[NEG:COLS].astype(BF)
    flush()
    pltpu.make_async_remote_copy(
        src_ref=others, dst_ref=others, send_sem=sst, recv_sem=rst1, device_id=sib, device_id_type=MESH
    ).wait_send()


def placed(held, oq, op, on, sem):
    copies = [
        pltpu.make_async_copy(held.at[pl.ds(0, ROWS)], oq, sem.at[0]),
        pltpu.make_async_copy(held.at[pl.ds(ROWS, ROWS)], op, sem.at[1]),
        pltpu.make_async_copy(held.at[pl.ds(2 * ROWS, NEG)], on, sem.at[2]),
    ]
    for cp in copies:
        cp.start()
    for cp in copies:
        cp.wait()


def on_device(queries, document_vectors, negatives, positives, neg_ids):
    dma = pltpu.SemaphoreType.DMA
    vm = pltpu.VMEM
    hbm = [
        pltpu.with_memory_space_constraint(a, pltpu.HBM)
        for a in (queries, document_vectors, negatives, positives.reshape(1, ROWS), neg_ids.T)
    ]
    out = pl.pallas_call(
        kernel,
        out_shape=pltpu.VMEM((2 * ROWS + NEG, D), BF),
        in_specs=[pl.BlockSpec(memory_space=pltpu.HBM)] * 5,
        scratch_shapes=[
            vm((1, ROWS), jnp.int32),
            vm((7, ROWS), jnp.int32),
            vm((128, 128), F32),
            vm((512, D + EXT), BF),
            vm((4 * COLS, D), BF),
            vm((4 * COLS, 512), F32),
            vm((4 * COLS, 512), BF),
            vm((4 * COLS, 512), F32),
            vm((256, D), BF),
            vm((256, D), F32),
            vm((256, D), BF),
            vm((256, D), BF),
            vm((64, D), BF),
            vm((64, D), BF),
            vm((2, 64, D), BF),
            vm((64, D), BF),
            vm((4, ROWS, D), BF),
            vm((COLS, D), BF),
            vm((2 * COLS, D), F32),
            vm((2 * COLS, D), BF),
            vm((COLS, D), F32),
            vm((COLS, D), BF),
            vm((COLS, D), BF),
            vm((COLS, D), BF),
            vm((32, 8, 128), F32),
            vm((8, 512), F32),
            dma((5,)),
            dma((3, NF)),
            dma((3, NF)),
            dma((4, 4)),
            dma((16,)),
            dma((32,)),
            dma,
            dma,
            dma((3, NF)),
            dma((NF,)),
            dma((NF,)),
            dma((NF,)),
            dma((NF,)),
            dma((NF,)),
            dma((3, 2, NF)),
            dma((2, NF)),
            dma((2, 2, NF)),
            dma((4, NF)),
            dma((4, NF)),
        ],
        compiler_params=pltpu.CompilerParams(
            collective_id=0, has_side_effects=True, vmem_limit_bytes=44 * 2**20
        ),
    )(*hbm)
    parts = ((0, ROWS), (ROWS, ROWS), (2 * ROWS, NEG))
    return pl.pallas_call(
        placed,
        out_shape=tuple(pltpu.HBM((n, D), BF) for _, n in parts),
        in_specs=[pl.BlockSpec(memory_space=pltpu.VMEM)],
        scratch_shapes=[dma((3,))],
    )(pltpu.with_memory_space_constraint(out, pltpu.VMEM))


def solution(mesh):
    rows = P(("blk", "grp"), None)
    return jax.shard_map(
        on_device,
        mesh=mesh,
        in_specs=(rows, rows, rows, P(("blk", "grp")), rows),
        out_specs=(rows, rows, rows),
        check_vma=False,
    )
```

```python
import jax
import jax.numpy as jnp
from jax import lax
from jax.experimental import pallas as pl
from jax.experimental.pallas import tpu as pltpu
from jax.sharding import PartitionSpec as P

MESH = pl.DeviceIdType.MESH
BF = jnp.bfloat16
F32 = jnp.float32
INV = 50.0
D = 4096
EXT = 128
NEG = 64
ROWS = 16
COLS = NEG + ROWS
CH = 2048
NF = D // CH
CX = 1024
NX = D // CX
HX = NX // 2
MIX = tuple(f for i in range(HX) for f in (i, i + HX))
FLOOR = -1e30


def kernel(
    q_in, p_in, n_in, pos_in, ids_in, out,
    PO, ID, E, Q, C, S, W, MU, sibs, ownq, rsib, G, rB2, gB, rB, T, rA, g3, g12, gsend, g0, rx2, rf1, rf2, st1, MT,
    lsem, sx, rx, sq, ssq, rq, sst, rst1, sg, rg2, rgf1, rgf2, ssib, rsibs, sB, rB2s, rBs, sA, rAs,
):
    b_id = lax.axis_index("blk")
    g_id = lax.axis_index("grp")
    x = b_id % 4
    y = (g_id // 8) * 2 + b_id // 4
    z = (g_id // 2) % 4
    c = g_id % 2

    def dev(xx, yy, zz, cc):
        xx, yy, zz = (xx + 4) % 4, (yy + 4) % 4, (zz + 4) % 4
        return {"blk": (yy % 2) * 4 + xx, "grp": ((yy // 2) * 4 + zz) * 2 + cc}

    right, left, sib = dev(x + 1, y, z, c), dev(x - 1, y, z, c), dev(x, y, z, 1 - c)
    A = z + c * (y - z)
    B = y + c * (z - y)

    def at(a, b):
        a, b = (a + 4) % 4, (b + 4) % 4
        return dev(x, b + c * (a - b), a + c * (b - a), c)

    def slot(cc, b, a):
        return cc * 16 + ((b + 4) % 4) * 4 + (a + 4) % 4

    def rows_of(s, count=ROWS):
        return pl.ds(pl.multiple_of(s * ROWS, ROWS), count)

    sent = []

    def send(src, dst, ss, rs, to):
        cp = pltpu.make_async_remote_copy(
            src_ref=src, dst_ref=dst, send_sem=ss, recv_sem=rs, device_id=to, device_id_type=MESH
        )
        cp.start()
        sent.append(cp)

    def flush():
        for cp in sent:
            cp.wait_send()
        sent.clear()

    def arrived(dst, rs):
        pltpu.make_async_remote_copy(
            src_ref=dst, dst_ref=dst, send_sem=lsem.at[0], recv_sem=rs, device_id=sib, device_id_type=MESH
        ).wait_recv()

    barrier = pltpu.get_barrier_semaphore()
    greet = [right, left, at(A + 2, B), at(A, B + 2), at(A + 1, B), at(A - 1, B), at(A, B + 1), at(A, B - 1), sib]
    for to in greet:
        pl.semaphore_signal(barrier, inc=1, device_id=to, device_id_type=MESH)
    mine = slot(c, B, A)
    own_rows = rows_of(mine)
    local = [
        pltpu.make_async_copy(n_in, C.at[pl.ds(0, NEG)], lsem.at[0]),
        pltpu.make_async_copy(p_in, C.at[pl.ds(NEG, ROWS)], lsem.at[1]),
        pltpu.make_async_copy(q_in, Q.at[own_rows, pl.ds(0, D)], lsem.at[2]),
        pltpu.make_async_copy(pos_in, PO, lsem.at[3]),
        pltpu.make_async_copy(ids_in, ID, lsem.at[4]),
    ]
    for cp in local:
        cp.start()
    E[...] = jnp.zeros((128, 128), F32)
    for cp in local:
        cp.wait()
    for r, part in ((0, ID[...]), (7, PO[...])):
        n = part.shape[0]
        E[r : r + n, 0:ROWS] = (part // 128).astype(F32)
        E[8 + r : 8 + r + n, 0:ROWS] = (part % 128).astype(F32)
    Q[own_rows, D : D + EXT] = jnp.transpose(E[...])[0:ROWS].astype(BF)
    pl.semaphore_wait(barrier, len(greet))

    def fcols(f):
        return pl.ds(f * CH, CH)

    def xcols(f):
        return pl.ds(f * CX, CX)

    def crows(k):
        return pl.ds(k * COLS, COLS)

    for f in range(NX):
        h = (f + HX) % NX
        send(C.at[crows(0), xcols(f)], C.at[crows(1), xcols(f)], sx.at[0, f], rx.at[0, f], right)
        send(C.at[crows(0), xcols(h)], C.at[crows(2), xcols(h)], sx.at[1, h], rx.at[1, h], left)
    for da in (1, 3, 2):
        send(Q.at[own_rows], Q.at[own_rows], sq.at[0, da], rq.at[mine], at(A + da, B))

    def to_sib(r, i):
        send(Q.at[rows_of(r)], Q.at[rows_of(r)], ssq.at[i], rq.at[r], sib)

    def spread(da):
        r = slot(c, B, A - da)
        rr = rows_of(r)
        if da:
            arrived(Q.at[rr], rq.at[r])
        for i, db in enumerate((1, -1)):
            send(Q.at[rr], Q.at[rr], sq.at[1 + i, da], rq.at[r], at(A, B + db))
        if da > 1:
            send(Q.at[rr], Q.at[rr], sq.at[3, da], rq.at[r], at(A, B + 2))
        to_sib(r, da)

    def pass_on(da):
        for i, db in enumerate((1, -1)):
            r = slot(c, B - db, A - da)
            rr = rows_of(r)
            arrived(Q.at[rr], rq.at[r])
            if da == i:
                send(Q.at[rr], Q.at[rr], sq.at[3, da], rq.at[r], at(A, B + db))
            to_sib(r, 4 + 4 * i + da)

    def columns_on(f):
        arrived(C.at[crows(1), xcols(f)], rx.at[0, f])
        send(C.at[crows(1), xcols(f)], C.at[crows(3), xcols(f)], sx.at[2, f], rx.at[2, f], right)
        h = f + HX
        arrived(C.at[crows(2), xcols(h)], rx.at[1, h])
        send(C.at[crows(2), xcols(h)], C.at[crows(3), xcols(h)], sx.at[2, h], rx.at[2, h], left)

    for da in (0, 1, 3):
        spread(da)
    pass_on(0)
    spread(2)
    columns_on(0)
    pass_on(1)
    pass_on(3)
    columns_on(1)
    pass_on(2)
    for da in (0, 1, 3, 2):
        r = slot(c, B + 2, A - da)
        arrived(Q.at[rows_of(r)], rq.at[r])
        to_sib(r, 12 + da)
    col_neg = lax.broadcasted_iota(jnp.int32, (NEG, 256), 0)
    col_pas = lax.broadcasted_iota(jnp.int32, (ROWS, 256), 0)

    def dots(lo, hi, rows, d0, d1):
        return INV * lax.dot_general(
            C[lo:hi, d0:d1], Q[rows, d0:d1], (((1,), (1,)), ((), ())), preferred_element_type=F32
        )

    def partial_stats(lo, hi, qs):
        for k in range(lo // COLS, hi // COLS):
            r0, r1 = k * COLS, k * COLS + NEG
            S[r0:r1, qs] = jnp.where(MU[r0:r1, qs] > 0.0, S[r0:r1, qs], FLOOR)
        m = jnp.max(S[lo:hi, qs], 0, keepdims=True)
        tot = jnp.zeros_like(m)
        for k in range(lo // COLS, hi // COLS):
            r0, r1, r2 = k * COLS, k * COLS + NEG, (k + 1) * COLS
            tot = tot + jnp.sum(jnp.exp(S[r0:r1, qs] - m) * MU[r0:r1, qs], 0, keepdims=True)
            tot = tot + jnp.sum(jnp.exp(S[r1:r2, qs] - m), 0, keepdims=True)
        return m, tot

    def half_scores(core):
        qs = pl.ds(pl.multiple_of(core * 256, 256), 256)
        ext = jnp.transpose(Q[qs, D : D + EXT].astype(F32))
        ids = ext[0:8] * 128.0 + ext[8:16]
        for k, dx in enumerate((0, 3, 1, 2)):
            lin = ((y % 2) * 4 + (x + dx) % 4) * 16 + g_id
            gid = (col_neg + lin * NEG).astype(F32)
            mult = jnp.zeros((NEG, 256), F32)
            for h in range(7):
                mult = mult + (ids[h : h + 1] == gid).astype(F32)
            MU[k * COLS : k * COLS + NEG, qs] = mult
            pid = (col_pas + lin * ROWS).astype(F32)
            MU[k * COLS + NEG : (k + 1) * COLS, qs] = (ids[7:8] == pid).astype(F32)
        S[0 : 3 * COLS, qs] = dots(0, 3 * COLS, qs, 0, D)
        m, tot = partial_stats(0, 3 * COLS, qs)
        MT[0:1, qs] = m
        MT[1:2, qs] = tot

    for f in range(HX):
        arrived(C.at[crows(1), xcols(f + HX)], rx.at[0, f + HX])
        arrived(C.at[crows(2), xcols(f)], rx.at[1, f])
    half_scores(c)
    for k in range(16):
        r = (1 - c) * 16 + k
        arrived(Q.at[rows_of(r)], rq.at[r])
    half_scores(1 - c)
    acc = jnp.zeros((COLS, 512), F32)
    for f in MIX:
        arrived(C.at[crows(3), xcols(f)], rx.at[2, f])
        acc = acc + dots(3 * COLS, 4 * COLS, slice(0, 512), f * CX, (f + 1) * CX)
    S[3 * COLS : 4 * COLS, :] = acc
    m_b, tot_b = partial_stats(3 * COLS, 4 * COLS, slice(0, 512))
    m_a, tot_a = MT[0:1, :], MT[1:2, :]

    m = jnp.maximum(m_a, m_b)
    tot = tot_a * jnp.exp(m_a - m) + tot_b * jnp.exp(m_b - m)
    for j in range(4):
        st1[0, j : j + 1, :] = m[:, j * 128 : (j + 1) * 128]
        st1[0, 4 + j : 5 + j, :] = tot[:, j * 128 : (j + 1) * 128]

    def merge(buf, n):
        top = buf[0, 0:4, :]
        for i in range(1, n):
            top = jnp.maximum(top, buf[i, 0:4, :])
        total = jnp.zeros((4, 128), F32)
        for i in range(n):
            total = total + buf[i, 4:8, :] * jnp.exp(buf[i, 0:4, :] - top)
        return top, total

    earlier = len(sent)
    for i in (*range(16, 24), *range(8, 16), *range(24, 32), *range(1, 8)):
        dy, dz, dc = i // 8, i // 2 % 4, i % 2
        send(st1.at[0], st1.at[i], sst, rst1, dev(x, y + dy, z + dz, (c + dc) % 2))
    del sent[earlier:]
    flush()
    others = st1.at[pl.ds(1, 31)]
    arrived(others, rst1)
    top, total = merge(st1, 32)
    lt = top + jnp.log(total)
    log_total = jnp.concatenate([lt[j : j + 1, :] for j in range(4)], 1)

    def weights(k):
        r0, r1, r2 = k * COLS, k * COLS + NEG, (k + 1) * COLS
        hard = jnp.exp(S[r0:r1, :] - log_total).astype(BF).astype(F32) * MU[r0:r1, :]
        W[r0:r1, :] = hard.astype(BF)
        W[r1:r2, :] = (jnp.exp(S[r1:r2, :] - log_total) - MU[r1:r2, :]).astype(BF)

    def col_grad(lo, hi, f):
        return INV * jnp.dot(W[lo:hi, :], Q[:, f * CX : (f + 1) * CX], preferred_element_type=F32)

    weights(3)
    for f in MIX:
        g3[:, f * CX : (f + 1) * CX] = col_grad(3 * COLS, 4 * COLS, f).astype(BF)
        to = right if f < HX else left
        send(g3.at[:, xcols(f)], rx2.at[:, xcols(f)], sg.at[0, f], rg2.at[f], to)
    for k in (0, 1, 2):
        weights(k)

    def query_grad(core, f):
        w = W[:, pl.ds(pl.multiple_of(core * 256, 256), 256)]
        return INV * lax.dot_general(
            w, C[:, f * CH : (f + 1) * CH], (((0,), (0,)), ((), ())), preferred_element_type=F32
        )

    def half(i):
        return pl.ds(32 * i, 32)

    def group(b, i):
        return rows_of(slot(0, b, 2 * i), 32)

    for f in MIX:
        cs = slice(f * CX, (f + 1) * CX)
        g12[:, cs] = col_grad(COLS, 3 * COLS, f)
        if f < HX:
            gsend[0:COLS, cs] = g12[0:COLS, cs].astype(BF)
            send(gsend.at[pl.ds(0, COLS), xcols(f)], rf2.at[:, xcols(f)], sg.at[1, f], rgf2.at[f], left)
        else:
            gsend[COLS:, cs] = g12[COLS:, cs].astype(BF)
            send(gsend.at[pl.ds(COLS, COLS), xcols(f)], rf1.at[:, xcols(f)], sg.at[1, f], rgf1.at[f], right)
    for f in range(NF):
        sibs[:, f * CH : (f + 1) * CH] = query_grad(1 - c, f).astype(BF)
        send(sibs.at[:, fcols(f)], rsib.at[:, fcols(f)], ssib.at[f], rsibs.at[f], sib)
    for f in range(NF):
        ownq[:, f * CH : (f + 1) * CH] = query_grad(c, f)
    for f in range(NF):
        cs = slice(f * CH, (f + 1) * CH)
        arrived(rsib.at[:, fcols(f)], rsibs.at[f])
        G[:, cs] = (ownq[:, cs] + rsib[:, cs].astype(F32)).astype(BF)
        for i, db in enumerate((1, -1)):
            h, o = half(i), half(1 - i)
            src = G.at[group(B + 2, i), fcols(f)]
            send(src, rB2.at[h, fcols(f)], sB.at[0, i, f], rB2s.at[i, f], at(A, B + db))
            src = G.at[group(B + db, 1 - i), fcols(f)]
            send(src, rB.at[i, o, fcols(f)], sB.at[1, i, f], rBs.at[i, 1 - i, f], at(A, B + db))
    for f in range(NF):
        cs = slice(f * CH, (f + 1) * CH)
        for i, db in enumerate((1, -1)):
            h = half(i)
            arrived(rB2.at[h, fcols(f)], rB2s.at[i, f])
            t = G[group(B + db, i), cs].astype(F32) + rB2[h, cs].astype(F32)
            gB[h, cs] = t.astype(BF)
            send(gB.at[h, fcols(f)], rB.at[i, h, fcols(f)], sB.at[2, i, f], rBs.at[i, i, f], at(A, B + db))
    for f in MIX:
        cs = slice(f * CX, (f + 1) * CX)
        arrived(rx2.at[:, xcols(f)], rg2.at[f])
        if f < HX:
            gsend[COLS:, cs] = (g12[COLS:, cs] + rx2[:, cs].astype(F32)).astype(BF)
            send(gsend.at[pl.ds(COLS, COLS), xcols(f)], rf1.at[:, xcols(f)], sg.at[2, f], rgf1.at[f], right)
        else:
            gsend[0:COLS, cs] = (g12[0:COLS, cs] + rx2[:, cs].astype(F32)).astype(BF)
            send(gsend.at[pl.ds(0, COLS), xcols(f)], rf2.at[:, xcols(f)], sg.at[2, f], rgf2.at[f], left)
    for f in range(NX):
        g0[:, f * CX : (f + 1) * CX] = col_grad(0, COLS, f)
    for f in range(NF):
        cs = slice(f * CH, (f + 1) * CH)
        t = G[rows_of(slot(0, B, 0), 64), cs].astype(F32)
        for i in range(2):
            for j in range(2):
                arrived(rB.at[i, half(j), fcols(f)], rBs.at[i, j, f])
            t = t + rB[i, :, cs].astype(F32)
        T[:, cs] = t.astype(BF)
        for da in (2, 1, 3):
            src = T.at[rows_of(slot(0, 0, A + da)), fcols(f)]
            send(src, rA.at[da, :, fcols(f)], sA.at[da, f], rAs.at[da, f], at(A + da, B))
    flush()
    for f in range(NF):
        cs = slice(f * CH, (f + 1) * CH)
        t = T[rows_of(A), cs].astype(F32)
        for da in (1, 2, 3):
            arrived(rA.at[da, :, fcols(f)], rAs.at[da, f])
            t = t + rA[da, :, cs].astype(F32)
        out[0:ROWS, cs] = t.astype(BF)
    for f in MIX:
        cs = slice(f * CX, (f + 1) * CX)
        arrived(rf1.at[:, xcols(f)], rgf1.at[f])
        arrived(rf2.at[:, xcols(f)], rgf2.at[f])
        t = g0[:, cs] + rf1[:, cs].astype(F32) + rf2[:, cs].astype(F32)
        out[2 * ROWS :, cs] = t[0:NEG].astype(BF)
        out[ROWS : 2 * ROWS, cs] = t[NEG:COLS].astype(BF)
    flush()
    pltpu.make_async_remote_copy(
        src_ref=others, dst_ref=others, send_sem=sst, recv_sem=rst1, device_id=sib, device_id_type=MESH
    ).wait_send()


def placed(held, oq, op, on, sem):
    copies = [
        pltpu.make_async_copy(held.at[pl.ds(0, ROWS)], oq, sem.at[0]),
        pltpu.make_async_copy(held.at[pl.ds(ROWS, ROWS)], op, sem.at[1]),
        pltpu.make_async_copy(held.at[pl.ds(2 * ROWS, NEG)], on, sem.at[2]),
    ]
    for cp in copies:
        cp.start()
    for cp in copies:
        cp.wait()


def on_device(queries, document_vectors, negatives, positives, neg_ids):
    dma = pltpu.SemaphoreType.DMA
    vm = pltpu.VMEM
    hbm = [
        pltpu.with_memory_space_constraint(a, pltpu.HBM)
        for a in (queries, document_vectors, negatives, positives.reshape(1, ROWS), neg_ids.T)
    ]
    out = pl.pallas_call(
        kernel,
        out_shape=pltpu.VMEM((2 * ROWS + NEG, D), BF),
        in_specs=[pl.BlockSpec(memory_space=pltpu.HBM)] * 5,
        scratch_shapes=[
            vm((1, ROWS), jnp.int32),
            vm((7, ROWS), jnp.int32),
            vm((128, 128), F32),
            vm((512, D + EXT), BF),
            vm((4 * COLS, D), BF),
            vm((4 * COLS, 512), F32),
            vm((4 * COLS, 512), BF),
            vm((4 * COLS, 512), F32),
            vm((256, D), BF),
            vm((256, D), F32),
            vm((256, D), BF),
            vm((256, D), BF),
            vm((64, D), BF),
            vm((64, D), BF),
            vm((2, 64, D), BF),
            vm((64, D), BF),
            vm((4, ROWS, D), BF),
            vm((COLS, D), BF),
            vm((2 * COLS, D), F32),
            vm((2 * COLS, D), BF),
            vm((COLS, D), F32),
            vm((COLS, D), BF),
            vm((COLS, D), BF),
            vm((COLS, D), BF),
            vm((32, 8, 128), F32),
            vm((8, 512), F32),
            dma((5,)),
            dma((3, NX)),
            dma((3, NX)),
            dma((4, 4)),
            dma((16,)),
            dma((32,)),
            dma,
            dma,
            dma((3, NX)),
            dma((NX,)),
            dma((NX,)),
            dma((NX,)),
            dma((NF,)),
            dma((NF,)),
            dma((3, 2, NF)),
            dma((2, NF)),
            dma((2, 2, NF)),
            dma((4, NF)),
            dma((4, NF)),
        ],
        compiler_params=pltpu.CompilerParams(
            collective_id=0, has_side_effects=True, vmem_limit_bytes=44 * 2**20
        ),
    )(*hbm)
    parts = ((0, ROWS), (ROWS, ROWS), (2 * ROWS, NEG))
    return pl.pallas_call(
        placed,
        out_shape=tuple(pltpu.HBM((n, D), BF) for _, n in parts),
        in_specs=[pl.BlockSpec(memory_space=pltpu.VMEM)],
        scratch_shapes=[dma((3,))],
    )(pltpu.with_memory_space_constraint(out, pltpu.VMEM))


def solution(mesh):
    rows = P(("blk", "grp"), None)
    return jax.shard_map(
        on_device,
        mesh=mesh,
        in_specs=(rows, rows, rows, P(("blk", "grp")), rows),
        out_specs=(rows, rows, rows),
        check_vma=False,
    )
```

```python
import jax
import jax.numpy as jnp
from jax import lax
from jax.experimental import pallas as pl
from jax.experimental.pallas import tpu as pltpu
from jax.sharding import PartitionSpec as P

MESH = pl.DeviceIdType.MESH
BF = jnp.bfloat16
F32 = jnp.float32
INV = 50.0
D = 4096
EXT = 128
NEG = 64
ROWS = 16
COLS = NEG + ROWS
CH = 2048
NF = D // CH
CX = 1024
NX = D // CX
HX = NX // 2
MIX = tuple(f for i in range(HX) for f in (i, i + HX))
GATHER = ((0, 1536), (1536, 512), (2048, 1536), (3584, 512))
FLOOR = -1e30


def kernel(
    q_in, p_in, n_in, pos_in, ids_in, out,
    PO, ID, E, Q, C, S, W, MU, sibs, ownq, rsib, G, rB2, gB, rB, T, rA, g3, g12, gsend, g0, rx2, rf1, rf2, st1, MT,
    lsem, sx, rx, sq, ssq, rq, sst, rst1, sg, rg2, rgf1, rgf2, ssib, rsibs, sB, rB2s, rBs, sA, rAs,
):
    b_id = lax.axis_index("blk")
    g_id = lax.axis_index("grp")
    x = b_id % 4
    y = (g_id // 8) * 2 + b_id // 4
    z = (g_id // 2) % 4
    c = g_id % 2

    def dev(xx, yy, zz, cc):
        xx, yy, zz = (xx + 4) % 4, (yy + 4) % 4, (zz + 4) % 4
        return {"blk": (yy % 2) * 4 + xx, "grp": ((yy // 2) * 4 + zz) * 2 + cc}

    right, left, sib = dev(x + 1, y, z, c), dev(x - 1, y, z, c), dev(x, y, z, 1 - c)
    A = z + c * (y - z)
    B = y + c * (z - y)

    def at(a, b):
        a, b = (a + 4) % 4, (b + 4) % 4
        return dev(x, b + c * (a - b), a + c * (b - a), c)

    def slot(cc, b, a):
        return cc * 16 + ((b + 4) % 4) * 4 + (a + 4) % 4

    def rows_of(s, count=ROWS):
        return pl.ds(pl.multiple_of(s * ROWS, ROWS), count)

    sent = []

    def send(src, dst, ss, rs, to):
        cp = pltpu.make_async_remote_copy(
            src_ref=src, dst_ref=dst, send_sem=ss, recv_sem=rs, device_id=to, device_id_type=MESH
        )
        cp.start()
        sent.append(cp)

    def flush():
        for cp in sent:
            cp.wait_send()
        sent.clear()

    def arrived(dst, rs):
        pltpu.make_async_remote_copy(
            src_ref=dst, dst_ref=dst, send_sem=lsem.at[0], recv_sem=rs, device_id=sib, device_id_type=MESH
        ).wait_recv()

    barrier = pltpu.get_barrier_semaphore()
    greet = [right, left, at(A + 2, B), at(A, B + 2), at(A + 1, B), at(A - 1, B), at(A, B + 1), at(A, B - 1), sib]
    for to in greet:
        pl.semaphore_signal(barrier, inc=1, device_id=to, device_id_type=MESH)
    mine = slot(c, B, A)
    own_rows = rows_of(mine)
    local = [
        pltpu.make_async_copy(n_in, C.at[pl.ds(0, NEG)], lsem.at[0]),
        pltpu.make_async_copy(p_in, C.at[pl.ds(NEG, ROWS)], lsem.at[1]),
        pltpu.make_async_copy(q_in, Q.at[own_rows, pl.ds(0, D)], lsem.at[2]),
        pltpu.make_async_copy(pos_in, PO, lsem.at[3]),
        pltpu.make_async_copy(ids_in, ID, lsem.at[4]),
    ]
    for cp in local:
        cp.start()
    local[0].wait()
    local[1].wait()
    pl.semaphore_wait(barrier, len(greet))

    def fcols(f):
        return pl.ds(f * CH, CH)

    def xcols(f):
        return pl.ds(f * CX, CX)

    def gcols(f):
        return pl.ds(*GATHER[f])

    def crows(k):
        return pl.ds(k * COLS, COLS)

    for f in range(NX):
        h = (f + HX) % NX
        send(C.at[crows(0), gcols(f)], C.at[crows(1), gcols(f)], sx.at[0, f], rx.at[0, f], right)
        send(C.at[crows(0), gcols(h)], C.at[crows(2), gcols(h)], sx.at[1, h], rx.at[1, h], left)
    E[...] = jnp.zeros((128, 128), F32)
    for cp in local[2:]:
        cp.wait()
    for r, part in ((0, ID[...]), (7, PO[...])):
        n = part.shape[0]
        E[r : r + n, 0:ROWS] = (part // 128).astype(F32)
        E[8 + r : 8 + r + n, 0:ROWS] = (part % 128).astype(F32)
    Q[own_rows, D : D + EXT] = jnp.transpose(E[...])[0:ROWS].astype(BF)
    for da in (1, 3, 2):
        send(Q.at[own_rows], Q.at[own_rows], sq.at[0, da], rq.at[mine], at(A + da, B))

    def to_sib(r, i):
        send(Q.at[rows_of(r)], Q.at[rows_of(r)], ssq.at[i], rq.at[r], sib)

    def spread(da):
        r = slot(c, B, A - da)
        rr = rows_of(r)
        if da:
            arrived(Q.at[rr], rq.at[r])
        for i, db in enumerate((1, -1)):
            send(Q.at[rr], Q.at[rr], sq.at[1 + i, da], rq.at[r], at(A, B + db))
        if da > 1:
            send(Q.at[rr], Q.at[rr], sq.at[3, da], rq.at[r], at(A, B + 2))
        to_sib(r, da)

    def pass_on(da):
        for i, db in enumerate((1, -1)):
            r = slot(c, B - db, A - da)
            rr = rows_of(r)
            arrived(Q.at[rr], rq.at[r])
            if da == i:
                send(Q.at[rr], Q.at[rr], sq.at[3, da], rq.at[r], at(A, B + db))
            to_sib(r, 4 + 4 * i + da)

    def columns_on(f):
        arrived(C.at[crows(1), gcols(f)], rx.at[0, f])
        send(C.at[crows(1), gcols(f)], C.at[crows(3), gcols(f)], sx.at[2, f], rx.at[2, f], right)
        h = f + HX
        arrived(C.at[crows(2), gcols(h)], rx.at[1, h])
        send(C.at[crows(2), gcols(h)], C.at[crows(3), gcols(h)], sx.at[2, h], rx.at[2, h], left)

    for da in (0, 1, 3):
        spread(da)
    pass_on(0)
    spread(2)
    columns_on(0)
    pass_on(1)
    pass_on(3)
    columns_on(1)
    pass_on(2)
    for da in (0, 1, 3, 2):
        r = slot(c, B + 2, A - da)
        arrived(Q.at[rows_of(r)], rq.at[r])
        to_sib(r, 12 + da)
    col_neg = lax.broadcasted_iota(jnp.int32, (NEG, 256), 0)
    col_pas = lax.broadcasted_iota(jnp.int32, (ROWS, 256), 0)

    def dots(lo, hi, rows, d0, d1):
        return INV * lax.dot_general(
            C[lo:hi, d0:d1], Q[rows, d0:d1], (((1,), (1,)), ((), ())), preferred_element_type=F32
        )

    def partial_stats(lo, hi, qs):
        for k in range(lo // COLS, hi // COLS):
            r0, r1 = k * COLS, k * COLS + NEG
            S[r0:r1, qs] = jnp.where(MU[r0:r1, qs] > 0.0, S[r0:r1, qs], FLOOR)
        m = jnp.max(S[lo:hi, qs], 0, keepdims=True)
        tot = jnp.zeros_like(m)
        for k in range(lo // COLS, hi // COLS):
            r0, r1, r2 = k * COLS, k * COLS + NEG, (k + 1) * COLS
            tot = tot + jnp.sum(jnp.exp(S[r0:r1, qs] - m) * MU[r0:r1, qs], 0, keepdims=True)
            tot = tot + jnp.sum(jnp.exp(S[r1:r2, qs] - m), 0, keepdims=True)
        return m, tot

    def half_scores(core):
        qs = pl.ds(pl.multiple_of(core * 256, 256), 256)
        ext = jnp.transpose(Q[qs, D : D + EXT].astype(F32))
        ids = ext[0:8] * 128.0 + ext[8:16]
        for k, dx in enumerate((0, 3, 1, 2)):
            lin = ((y % 2) * 4 + (x + dx) % 4) * 16 + g_id
            gid = (col_neg + lin * NEG).astype(F32)
            mult = jnp.zeros((NEG, 256), F32)
            for h in range(7):
                mult = mult + (ids[h : h + 1] == gid).astype(F32)
            MU[k * COLS : k * COLS + NEG, qs] = mult
            pid = (col_pas + lin * ROWS).astype(F32)
            MU[k * COLS + NEG : (k + 1) * COLS, qs] = (ids[7:8] == pid).astype(F32)
        S[0 : 3 * COLS, qs] = dots(0, 3 * COLS, qs, 0, D)
        m, tot = partial_stats(0, 3 * COLS, qs)
        MT[0:1, qs] = m
        MT[1:2, qs] = tot

    for f in range(HX):
        arrived(C.at[crows(1), gcols(f + HX)], rx.at[0, f + HX])
        arrived(C.at[crows(2), gcols(f)], rx.at[1, f])
    half_scores(c)
    for k in range(16):
        r = (1 - c) * 16 + k
        arrived(Q.at[rows_of(r)], rq.at[r])
    half_scores(1 - c)
    acc = jnp.zeros((COLS, 512), F32)
    for f in MIX:
        arrived(C.at[crows(3), gcols(f)], rx.at[2, f])
        acc = acc + dots(3 * COLS, 4 * COLS, slice(0, 512), GATHER[f][0], sum(GATHER[f]))
    S[3 * COLS : 4 * COLS, :] = acc
    m_b, tot_b = partial_stats(3 * COLS, 4 * COLS, slice(0, 512))
    m_a, tot_a = MT[0:1, :], MT[1:2, :]

    m = jnp.maximum(m_a, m_b)
    tot = tot_a * jnp.exp(m_a - m) + tot_b * jnp.exp(m_b - m)
    for j in range(4):
        st1[0, j : j + 1, :] = m[:, j * 128 : (j + 1) * 128]
        st1[0, 4 + j : 5 + j, :] = tot[:, j * 128 : (j + 1) * 128]

    def merge(buf, n):
        top = buf[0, 0:4, :]
        for i in range(1, n):
            top = jnp.maximum(top, buf[i, 0:4, :])
        total = jnp.zeros((4, 128), F32)
        for i in range(n):
            total = total + buf[i, 4:8, :] * jnp.exp(buf[i, 0:4, :] - top)
        return top, total

    earlier = len(sent)
    for i in (*range(16, 24), *range(8, 16), *range(24, 32), *range(1, 8)):
        dy, dz, dc = i // 8, i // 2 % 4, i % 2
        send(st1.at[0], st1.at[i], sst, rst1, dev(x, y + dy, z + dz, (c + dc) % 2))
    del sent[earlier:]
    flush()
    others = st1.at[pl.ds(1, 31)]
    arrived(others, rst1)
    top, total = merge(st1, 32)
    lt = top + jnp.log(total)
    log_total = jnp.concatenate([lt[j : j + 1, :] for j in range(4)], 1)

    def weights(k):
        r0, r1, r2 = k * COLS, k * COLS + NEG, (k + 1) * COLS
        hard = jnp.exp(S[r0:r1, :] - log_total).astype(BF).astype(F32) * MU[r0:r1, :]
        W[r0:r1, :] = hard.astype(BF)
        W[r1:r2, :] = (jnp.exp(S[r1:r2, :] - log_total) - MU[r1:r2, :]).astype(BF)

    def col_grad(lo, hi, f):
        return INV * jnp.dot(W[lo:hi, :], Q[:, f * CX : (f + 1) * CX], preferred_element_type=F32)

    weights(3)
    for f in MIX:
        g3[:, f * CX : (f + 1) * CX] = col_grad(3 * COLS, 4 * COLS, f).astype(BF)
        to = right if f < HX else left
        send(g3.at[:, xcols(f)], rx2.at[:, xcols(f)], sg.at[0, f], rg2.at[f], to)
    for k in (0, 1, 2):
        weights(k)

    def query_grad(core, f):
        w = W[:, pl.ds(pl.multiple_of(core * 256, 256), 256)]
        return INV * lax.dot_general(
            w, C[:, f * CH : (f + 1) * CH], (((0,), (0,)), ((), ())), preferred_element_type=F32
        )

    def half(i):
        return pl.ds(32 * i, 32)

    def group(b, i):
        return rows_of(slot(0, b, 2 * i), 32)

    for f in MIX:
        cs = slice(f * CX, (f + 1) * CX)
        g12[:, cs] = col_grad(COLS, 3 * COLS, f)
        if f < HX:
            gsend[0:COLS, cs] = g12[0:COLS, cs].astype(BF)
            send(gsend.at[pl.ds(0, COLS), xcols(f)], rf2.at[:, xcols(f)], sg.at[1, f], rgf2.at[f], left)
        else:
            gsend[COLS:, cs] = g12[COLS:, cs].astype(BF)
            send(gsend.at[pl.ds(COLS, COLS), xcols(f)], rf1.at[:, xcols(f)], sg.at[1, f], rgf1.at[f], right)
    for f in range(NF):
        sibs[:, f * CH : (f + 1) * CH] = query_grad(1 - c, f).astype(BF)
        send(sibs.at[:, fcols(f)], rsib.at[:, fcols(f)], ssib.at[f], rsibs.at[f], sib)
    for f in range(NF):
        ownq[:, f * CH : (f + 1) * CH] = query_grad(c, f)
    for f in range(NF):
        cs = slice(f * CH, (f + 1) * CH)
        arrived(rsib.at[:, fcols(f)], rsibs.at[f])
        G[:, cs] = (ownq[:, cs] + rsib[:, cs].astype(F32)).astype(BF)
        for i, db in enumerate((1, -1)):
            h, o = half(i), half(1 - i)
            src = G.at[group(B + 2, i), fcols(f)]
            send(src, rB2.at[h, fcols(f)], sB.at[0, i, f], rB2s.at[i, f], at(A, B + db))
            src = G.at[group(B + db, 1 - i), fcols(f)]
            send(src, rB.at[i, o, fcols(f)], sB.at[1, i, f], rBs.at[i, 1 - i, f], at(A, B + db))
    for f in range(NF):
        cs = slice(f * CH, (f + 1) * CH)
        for i, db in enumerate((1, -1)):
            h = half(i)
            arrived(rB2.at[h, fcols(f)], rB2s.at[i, f])
            t = G[group(B + db, i), cs].astype(F32) + rB2[h, cs].astype(F32)
            gB[h, cs] = t.astype(BF)
            send(gB.at[h, fcols(f)], rB.at[i, h, fcols(f)], sB.at[2, i, f], rBs.at[i, i, f], at(A, B + db))
    for f in MIX:
        cs = slice(f * CX, (f + 1) * CX)
        arrived(rx2.at[:, xcols(f)], rg2.at[f])
        if f < HX:
            gsend[COLS:, cs] = (g12[COLS:, cs] + rx2[:, cs].astype(F32)).astype(BF)
            send(gsend.at[pl.ds(COLS, COLS), xcols(f)], rf1.at[:, xcols(f)], sg.at[2, f], rgf1.at[f], right)
        else:
            gsend[0:COLS, cs] = (g12[0:COLS, cs] + rx2[:, cs].astype(F32)).astype(BF)
            send(gsend.at[pl.ds(0, COLS), xcols(f)], rf2.at[:, xcols(f)], sg.at[2, f], rgf2.at[f], left)
    for f in range(NX):
        g0[:, f * CX : (f + 1) * CX] = col_grad(0, COLS, f)
    for f in range(NF):
        cs = slice(f * CH, (f + 1) * CH)
        t = G[rows_of(slot(0, B, 0), 64), cs].astype(F32)
        for i in range(2):
            for j in range(2):
                arrived(rB.at[i, half(j), fcols(f)], rBs.at[i, j, f])
            t = t + rB[i, :, cs].astype(F32)
        T[:, cs] = t.astype(BF)
        for da in (2, 1, 3):
            src = T.at[rows_of(slot(0, 0, A + da)), fcols(f)]
            send(src, rA.at[da, :, fcols(f)], sA.at[da, f], rAs.at[da, f], at(A + da, B))
    flush()
    for f in range(NF):
        cs = slice(f * CH, (f + 1) * CH)
        t = T[rows_of(A), cs].astype(F32)
        for da in (1, 2, 3):
            arrived(rA.at[da, :, fcols(f)], rAs.at[da, f])
            t = t + rA[da, :, cs].astype(F32)
        out[0:ROWS, cs] = t.astype(BF)
    for f in MIX:
        cs = slice(f * CX, (f + 1) * CX)
        arrived(rf1.at[:, xcols(f)], rgf1.at[f])
        arrived(rf2.at[:, xcols(f)], rgf2.at[f])
        t = g0[:, cs] + rf1[:, cs].astype(F32) + rf2[:, cs].astype(F32)
        out[2 * ROWS :, cs] = t[0:NEG].astype(BF)
        out[ROWS : 2 * ROWS, cs] = t[NEG:COLS].astype(BF)
    flush()
    pltpu.make_async_remote_copy(
        src_ref=others, dst_ref=others, send_sem=sst, recv_sem=rst1, device_id=sib, device_id_type=MESH
    ).wait_send()


def placed(held, oq, op, on, sem):
    copies = [
        pltpu.make_async_copy(held.at[pl.ds(0, ROWS)], oq, sem.at[0]),
        pltpu.make_async_copy(held.at[pl.ds(ROWS, ROWS)], op, sem.at[1]),
        pltpu.make_async_copy(held.at[pl.ds(2 * ROWS, NEG)], on, sem.at[2]),
    ]
    for cp in copies:
        cp.start()
    for cp in copies:
        cp.wait()


def on_device(queries, document_vectors, negatives, positives, neg_ids):
    dma = pltpu.SemaphoreType.DMA
    vm = pltpu.VMEM
    hbm = [
        pltpu.with_memory_space_constraint(a, pltpu.HBM)
        for a in (queries, document_vectors, negatives, positives.reshape(1, ROWS), neg_ids.T)
    ]
    out = pl.pallas_call(
        kernel,
        out_shape=pltpu.VMEM((2 * ROWS + NEG, D), BF),
        in_specs=[pl.BlockSpec(memory_space=pltpu.HBM)] * 5,
        scratch_shapes=[
            vm((1, ROWS), jnp.int32),
            vm((7, ROWS), jnp.int32),
            vm((128, 128), F32),
            vm((512, D + EXT), BF),
            vm((4 * COLS, D), BF),
            vm((4 * COLS, 512), F32),
            vm((4 * COLS, 512), BF),
            vm((4 * COLS, 512), F32),
            vm((256, D), BF),
            vm((256, D), F32),
            vm((256, D), BF),
            vm((256, D), BF),
            vm((64, D), BF),
            vm((64, D), BF),
            vm((2, 64, D), BF),
            vm((64, D), BF),
            vm((4, ROWS, D), BF),
            vm((COLS, D), BF),
            vm((2 * COLS, D), F32),
            vm((2 * COLS, D), BF),
            vm((COLS, D), F32),
            vm((COLS, D), BF),
            vm((COLS, D), BF),
            vm((COLS, D), BF),
            vm((32, 8, 128), F32),
            vm((8, 512), F32),
            dma((5,)),
            dma((3, NX)),
            dma((3, NX)),
            dma((4, 4)),
            dma((16,)),
            dma((32,)),
            dma,
            dma,
            dma((3, NX)),
            dma((NX,)),
            dma((NX,)),
            dma((NX,)),
            dma((NF,)),
            dma((NF,)),
            dma((3, 2, NF)),
            dma((2, NF)),
            dma((2, 2, NF)),
            dma((4, NF)),
            dma((4, NF)),
        ],
        compiler_params=pltpu.CompilerParams(
            collective_id=0, has_side_effects=True, vmem_limit_bytes=44 * 2**20
        ),
    )(*hbm)
    parts = ((0, ROWS), (ROWS, ROWS), (2 * ROWS, NEG))
    return pl.pallas_call(
        placed,
        out_shape=tuple(pltpu.HBM((n, D), BF) for _, n in parts),
        in_specs=[pl.BlockSpec(memory_space=pltpu.VMEM)],
        scratch_shapes=[dma((3,))],
    )(pltpu.with_memory_space_constraint(out, pltpu.VMEM))


def solution(mesh):
    rows = P(("blk", "grp"), None)
    return jax.shard_map(
        on_device,
        mesh=mesh,
        in_specs=(rows, rows, rows, P(("blk", "grp")), rows),
        out_specs=(rows, rows, rows),
        check_vma=False,
    )
```

```python
import jax
import jax.numpy as jnp
from jax import lax
from jax.experimental import pallas as pl
from jax.experimental.pallas import tpu as pltpu
from jax.sharding import PartitionSpec as P

MESH = pl.DeviceIdType.MESH
BF = jnp.bfloat16
F32 = jnp.float32
INV = 50.0
D = 4096
EXT = 128
NEG = 64
ROWS = 16
COLS = NEG + ROWS
CH = 2048
NF = D // CH
CX = 1024
NX = D // CX
HX = NX // 2
MIX = tuple(f for i in range(HX) for f in (i, i + HX))
GATHER = ((0, 1536), (1536, 512), (2048, 1536), (3584, 512))
FLOOR = -1e30
RETURN = ((0, 512), (512, 1536), (2048, 512), (2560, 1536))


def kernel(
    q_in, p_in, n_in, pos_in, ids_in, out,
    PO, ID, E, Q, C, S, W, MU, sibs, ownq, rsib, G, rB2, gB, rB, T, rA, g3, g12, gsend, g0, rx2, rf1, rf2, st1, MT,
    lsem, sx, rx, sq, ssq, rq, sst, rst1, sg, rg2, rgf1, rgf2, ssib, rsibs, sB, rB2s, rBs, sA, rAs,
):
    b_id = lax.axis_index("blk")
    g_id = lax.axis_index("grp")
    x = b_id % 4
    y = (g_id // 8) * 2 + b_id // 4
    z = (g_id // 2) % 4
    c = g_id % 2

    def dev(xx, yy, zz, cc):
        xx, yy, zz = (xx + 4) % 4, (yy + 4) % 4, (zz + 4) % 4
        return {"blk": (yy % 2) * 4 + xx, "grp": ((yy // 2) * 4 + zz) * 2 + cc}

    right, left, sib = dev(x + 1, y, z, c), dev(x - 1, y, z, c), dev(x, y, z, 1 - c)
    A = z + c * (y - z)
    B = y + c * (z - y)

    def at(a, b):
        a, b = (a + 4) % 4, (b + 4) % 4
        return dev(x, b + c * (a - b), a + c * (b - a), c)

    def slot(cc, b, a):
        return cc * 16 + ((b + 4) % 4) * 4 + (a + 4) % 4

    def rows_of(s, count=ROWS):
        return pl.ds(pl.multiple_of(s * ROWS, ROWS), count)

    sent = []

    def send(src, dst, ss, rs, to):
        cp = pltpu.make_async_remote_copy(
            src_ref=src, dst_ref=dst, send_sem=ss, recv_sem=rs, device_id=to, device_id_type=MESH
        )
        cp.start()
        sent.append(cp)

    def flush():
        for cp in sent:
            cp.wait_send()
        sent.clear()

    def arrived(dst, rs):
        pltpu.make_async_remote_copy(
            src_ref=dst, dst_ref=dst, send_sem=lsem.at[0], recv_sem=rs, device_id=sib, device_id_type=MESH
        ).wait_recv()

    barrier = pltpu.get_barrier_semaphore()
    greet = [right, left, at(A + 2, B), at(A, B + 2), at(A + 1, B), at(A - 1, B), at(A, B + 1), at(A, B - 1), sib]
    for to in greet:
        pl.semaphore_signal(barrier, inc=1, device_id=to, device_id_type=MESH)
    mine = slot(c, B, A)
    own_rows = rows_of(mine)
    local = [
        pltpu.make_async_copy(n_in, C.at[pl.ds(0, NEG)], lsem.at[0]),
        pltpu.make_async_copy(p_in, C.at[pl.ds(NEG, ROWS)], lsem.at[1]),
        pltpu.make_async_copy(q_in, Q.at[own_rows, pl.ds(0, D)], lsem.at[2]),
        pltpu.make_async_copy(pos_in, PO, lsem.at[3]),
        pltpu.make_async_copy(ids_in, ID, lsem.at[4]),
    ]
    for cp in local:
        cp.start()
    local[0].wait()
    local[1].wait()
    pl.semaphore_wait(barrier, len(greet))

    def fcols(f):
        return pl.ds(f * CH, CH)

    def gcols(f):
        return pl.ds(*GATHER[f])

    def scols(f):
        return pl.ds(*RETURN[f])

    def crows(k):
        return pl.ds(k * COLS, COLS)

    for f in range(NX):
        h = (f + HX) % NX
        send(C.at[crows(0), gcols(f)], C.at[crows(1), gcols(f)], sx.at[0, f], rx.at[0, f], right)
        send(C.at[crows(0), gcols(h)], C.at[crows(2), gcols(h)], sx.at[1, h], rx.at[1, h], left)
    E[...] = jnp.zeros((128, 128), F32)
    for cp in local[2:]:
        cp.wait()
    for r, part in ((0, ID[...]), (7, PO[...])):
        n = part.shape[0]
        E[r : r + n, 0:ROWS] = (part // 128).astype(F32)
        E[8 + r : 8 + r + n, 0:ROWS] = (part % 128).astype(F32)
    Q[own_rows, D : D + EXT] = jnp.transpose(E[...])[0:ROWS].astype(BF)
    for da in (1, 3, 2):
        send(Q.at[own_rows], Q.at[own_rows], sq.at[0, da], rq.at[mine], at(A + da, B))

    def to_sib(r, i):
        send(Q.at[rows_of(r)], Q.at[rows_of(r)], ssq.at[i], rq.at[r], sib)

    def spread(da):
        r = slot(c, B, A - da)
        rr = rows_of(r)
        if da:
            arrived(Q.at[rr], rq.at[r])
        for i, db in enumerate((1, -1)):
            send(Q.at[rr], Q.at[rr], sq.at[1 + i, da], rq.at[r], at(A, B + db))
        if da > 1:
            send(Q.at[rr], Q.at[rr], sq.at[3, da], rq.at[r], at(A, B + 2))
        to_sib(r, da)

    def pass_on(da):
        for i, db in enumerate((1, -1)):
            r = slot(c, B - db, A - da)
            rr = rows_of(r)
            arrived(Q.at[rr], rq.at[r])
            if da == i:
                send(Q.at[rr], Q.at[rr], sq.at[3, da], rq.at[r], at(A, B + db))
            to_sib(r, 4 + 4 * i + da)

    def columns_on(f):
        arrived(C.at[crows(1), gcols(f)], rx.at[0, f])
        send(C.at[crows(1), gcols(f)], C.at[crows(3), gcols(f)], sx.at[2, f], rx.at[2, f], right)
        h = f + HX
        arrived(C.at[crows(2), gcols(h)], rx.at[1, h])
        send(C.at[crows(2), gcols(h)], C.at[crows(3), gcols(h)], sx.at[2, h], rx.at[2, h], left)

    for da in (0, 1, 3):
        spread(da)
    pass_on(0)
    spread(2)
    columns_on(0)
    pass_on(1)
    pass_on(3)
    columns_on(1)
    pass_on(2)
    for da in (0, 1, 3, 2):
        r = slot(c, B + 2, A - da)
        arrived(Q.at[rows_of(r)], rq.at[r])
        to_sib(r, 12 + da)
    col_neg = lax.broadcasted_iota(jnp.int32, (NEG, 256), 0)
    col_pas = lax.broadcasted_iota(jnp.int32, (ROWS, 256), 0)

    def dots(lo, hi, rows, d0, d1):
        return INV * lax.dot_general(
            C[lo:hi, d0:d1], Q[rows, d0:d1], (((1,), (1,)), ((), ())), preferred_element_type=F32
        )

    def partial_stats(lo, hi, qs):
        for k in range(lo // COLS, hi // COLS):
            r0, r1 = k * COLS, k * COLS + NEG
            S[r0:r1, qs] = jnp.where(MU[r0:r1, qs] > 0.0, S[r0:r1, qs], FLOOR)
        m = jnp.max(S[lo:hi, qs], 0, keepdims=True)
        tot = jnp.zeros_like(m)
        for k in range(lo // COLS, hi // COLS):
            r0, r1, r2 = k * COLS, k * COLS + NEG, (k + 1) * COLS
            tot = tot + jnp.sum(jnp.exp(S[r0:r1, qs] - m) * MU[r0:r1, qs], 0, keepdims=True)
            tot = tot + jnp.sum(jnp.exp(S[r1:r2, qs] - m), 0, keepdims=True)
        return m, tot

    def half_scores(core):
        qs = pl.ds(pl.multiple_of(core * 256, 256), 256)
        ext = jnp.transpose(Q[qs, D : D + EXT].astype(F32))
        ids = ext[0:8] * 128.0 + ext[8:16]
        for k, dx in enumerate((0, 3, 1, 2)):
            lin = ((y % 2) * 4 + (x + dx) % 4) * 16 + g_id
            gid = (col_neg + lin * NEG).astype(F32)
            mult = jnp.zeros((NEG, 256), F32)
            for h in range(7):
                mult = mult + (ids[h : h + 1] == gid).astype(F32)
            MU[k * COLS : k * COLS + NEG, qs] = mult
            pid = (col_pas + lin * ROWS).astype(F32)
            MU[k * COLS + NEG : (k + 1) * COLS, qs] = (ids[7:8] == pid).astype(F32)
        S[0 : 3 * COLS, qs] = dots(0, 3 * COLS, qs, 0, D)
        m, tot = partial_stats(0, 3 * COLS, qs)
        MT[0:1, qs] = m
        MT[1:2, qs] = tot

    for f in range(HX):
        arrived(C.at[crows(1), gcols(f + HX)], rx.at[0, f + HX])
        arrived(C.at[crows(2), gcols(f)], rx.at[1, f])
    half_scores(c)
    for k in range(16):
        r = (1 - c) * 16 + k
        arrived(Q.at[rows_of(r)], rq.at[r])
    half_scores(1 - c)
    acc = jnp.zeros((COLS, 512), F32)
    for f in MIX:
        arrived(C.at[crows(3), gcols(f)], rx.at[2, f])
        acc = acc + dots(3 * COLS, 4 * COLS, slice(0, 512), GATHER[f][0], sum(GATHER[f]))
    S[3 * COLS : 4 * COLS, :] = acc
    m_b, tot_b = partial_stats(3 * COLS, 4 * COLS, slice(0, 512))
    m_a, tot_a = MT[0:1, :], MT[1:2, :]

    m = jnp.maximum(m_a, m_b)
    tot = tot_a * jnp.exp(m_a - m) + tot_b * jnp.exp(m_b - m)
    for j in range(4):
        st1[0, j : j + 1, :] = m[:, j * 128 : (j + 1) * 128]
        st1[0, 4 + j : 5 + j, :] = tot[:, j * 128 : (j + 1) * 128]

    def merge(buf, n):
        top = buf[0, 0:4, :]
        for i in range(1, n):
            top = jnp.maximum(top, buf[i, 0:4, :])
        total = jnp.zeros((4, 128), F32)
        for i in range(n):
            total = total + buf[i, 4:8, :] * jnp.exp(buf[i, 0:4, :] - top)
        return top, total

    earlier = len(sent)
    for i in (*range(16, 24), *range(8, 16), *range(24, 32), *range(1, 8)):
        dy, dz, dc = i // 8, i // 2 % 4, i % 2
        send(st1.at[0], st1.at[i], sst, rst1, dev(x, y + dy, z + dz, (c + dc) % 2))
    del sent[earlier:]
    flush()
    others = st1.at[pl.ds(1, 31)]
    arrived(others, rst1)
    top, total = merge(st1, 32)
    lt = top + jnp.log(total)
    log_total = jnp.concatenate([lt[j : j + 1, :] for j in range(4)], 1)

    def weights(k):
        r0, r1, r2 = k * COLS, k * COLS + NEG, (k + 1) * COLS
        hard = jnp.exp(S[r0:r1, :] - log_total).astype(BF).astype(F32) * MU[r0:r1, :]
        W[r0:r1, :] = hard.astype(BF)
        W[r1:r2, :] = (jnp.exp(S[r1:r2, :] - log_total) - MU[r1:r2, :]).astype(BF)

    def col_grad(lo, hi, f):
        return INV * jnp.dot(W[lo:hi, :], Q[:, RETURN[f][0] : sum(RETURN[f])], preferred_element_type=F32)

    weights(3)
    for f in MIX:
        g3[:, RETURN[f][0] : sum(RETURN[f])] = col_grad(3 * COLS, 4 * COLS, f).astype(BF)
        to = right if f < HX else left
        send(g3.at[:, scols(f)], rx2.at[:, scols(f)], sg.at[0, f], rg2.at[f], to)
    for k in (0, 1, 2):
        weights(k)

    def query_grad(core, f):
        w = W[:, pl.ds(pl.multiple_of(core * 256, 256), 256)]
        return INV * lax.dot_general(
            w, C[:, f * CH : (f + 1) * CH], (((0,), (0,)), ((), ())), preferred_element_type=F32
        )

    def half(i):
        return pl.ds(32 * i, 32)

    def group(b, i):
        return rows_of(slot(0, b, 2 * i), 32)

    for f in MIX:
        cs = slice(RETURN[f][0], sum(RETURN[f]))
        g12[:, cs] = col_grad(COLS, 3 * COLS, f)
        if f < HX:
            gsend[0:COLS, cs] = g12[0:COLS, cs].astype(BF)
            send(gsend.at[pl.ds(0, COLS), scols(f)], rf2.at[:, scols(f)], sg.at[1, f], rgf2.at[f], left)
        else:
            gsend[COLS:, cs] = g12[COLS:, cs].astype(BF)
            send(gsend.at[pl.ds(COLS, COLS), scols(f)], rf1.at[:, scols(f)], sg.at[1, f], rgf1.at[f], right)
    for f in range(NF):
        sibs[:, f * CH : (f + 1) * CH] = query_grad(1 - c, f).astype(BF)
        send(sibs.at[:, fcols(f)], rsib.at[:, fcols(f)], ssib.at[f], rsibs.at[f], sib)
    for f in range(NF):
        ownq[:, f * CH : (f + 1) * CH] = query_grad(c, f)
    for f in range(NF):
        cs = slice(f * CH, (f + 1) * CH)
        arrived(rsib.at[:, fcols(f)], rsibs.at[f])
        G[:, cs] = (ownq[:, cs] + rsib[:, cs].astype(F32)).astype(BF)
        for i, db in enumerate((1, -1)):
            h, o = half(i), half(1 - i)
            src = G.at[group(B + 2, i), fcols(f)]
            send(src, rB2.at[h, fcols(f)], sB.at[0, i, f], rB2s.at[i, f], at(A, B + db))
            src = G.at[group(B + db, 1 - i), fcols(f)]
            send(src, rB.at[i, o, fcols(f)], sB.at[1, i, f], rBs.at[i, 1 - i, f], at(A, B + db))
    for f in range(NF):
        cs = slice(f * CH, (f + 1) * CH)
        for i, db in enumerate((1, -1)):
            h = half(i)
            arrived(rB2.at[h, fcols(f)], rB2s.at[i, f])
            t = G[group(B + db, i), cs].astype(F32) + rB2[h, cs].astype(F32)
            gB[h, cs] = t.astype(BF)
            send(gB.at[h, fcols(f)], rB.at[i, h, fcols(f)], sB.at[2, i, f], rBs.at[i, i, f], at(A, B + db))
    for f in MIX:
        cs = slice(RETURN[f][0], sum(RETURN[f]))
        arrived(rx2.at[:, scols(f)], rg2.at[f])
        if f < HX:
            gsend[COLS:, cs] = (g12[COLS:, cs] + rx2[:, cs].astype(F32)).astype(BF)
            send(gsend.at[pl.ds(COLS, COLS), scols(f)], rf1.at[:, scols(f)], sg.at[2, f], rgf1.at[f], right)
        else:
            gsend[0:COLS, cs] = (g12[0:COLS, cs] + rx2[:, cs].astype(F32)).astype(BF)
            send(gsend.at[pl.ds(0, COLS), scols(f)], rf2.at[:, scols(f)], sg.at[2, f], rgf2.at[f], left)
    for f in range(NX):
        g0[:, RETURN[f][0] : sum(RETURN[f])] = col_grad(0, COLS, f)
    for f in range(NF):
        cs = slice(f * CH, (f + 1) * CH)
        t = G[rows_of(slot(0, B, 0), 64), cs].astype(F32)
        for i in range(2):
            for j in range(2):
                arrived(rB.at[i, half(j), fcols(f)], rBs.at[i, j, f])
            t = t + rB[i, :, cs].astype(F32)
        T[:, cs] = t.astype(BF)
        for da in (2, 1, 3):
            src = T.at[rows_of(slot(0, 0, A + da)), fcols(f)]
            send(src, rA.at[da, :, fcols(f)], sA.at[da, f], rAs.at[da, f], at(A + da, B))
    flush()
    for f in range(NF):
        cs = slice(f * CH, (f + 1) * CH)
        t = T[rows_of(A), cs].astype(F32)
        for da in (1, 2, 3):
            arrived(rA.at[da, :, fcols(f)], rAs.at[da, f])
            t = t + rA[da, :, cs].astype(F32)
        out[0:ROWS, cs] = t.astype(BF)
    for f in MIX:
        cs = slice(RETURN[f][0], sum(RETURN[f]))
        arrived(rf1.at[:, scols(f)], rgf1.at[f])
        arrived(rf2.at[:, scols(f)], rgf2.at[f])
        t = g0[:, cs] + rf1[:, cs].astype(F32) + rf2[:, cs].astype(F32)
        out[2 * ROWS :, cs] = t[0:NEG].astype(BF)
        out[ROWS : 2 * ROWS, cs] = t[NEG:COLS].astype(BF)
    flush()
    pltpu.make_async_remote_copy(
        src_ref=others, dst_ref=others, send_sem=sst, recv_sem=rst1, device_id=sib, device_id_type=MESH
    ).wait_send()


def placed(held, oq, op, on, sem):
    copies = [
        pltpu.make_async_copy(held.at[pl.ds(0, ROWS)], oq, sem.at[0]),
        pltpu.make_async_copy(held.at[pl.ds(ROWS, ROWS)], op, sem.at[1]),
        pltpu.make_async_copy(held.at[pl.ds(2 * ROWS, NEG)], on, sem.at[2]),
    ]
    for cp in copies:
        cp.start()
    for cp in copies:
        cp.wait()


def on_device(queries, document_vectors, negatives, positives, neg_ids):
    dma = pltpu.SemaphoreType.DMA
    vm = pltpu.VMEM
    hbm = [
        pltpu.with_memory_space_constraint(a, pltpu.HBM)
        for a in (queries, document_vectors, negatives, positives.reshape(1, ROWS), neg_ids.T)
    ]
    out = pl.pallas_call(
        kernel,
        out_shape=pltpu.VMEM((2 * ROWS + NEG, D), BF),
        in_specs=[pl.BlockSpec(memory_space=pltpu.HBM)] * 5,
        scratch_shapes=[
            vm((1, ROWS), jnp.int32),
            vm((7, ROWS), jnp.int32),
            vm((128, 128), F32),
            vm((512, D + EXT), BF),
            vm((4 * COLS, D), BF),
            vm((4 * COLS, 512), F32),
            vm((4 * COLS, 512), BF),
            vm((4 * COLS, 512), F32),
            vm((256, D), BF),
            vm((256, D), F32),
            vm((256, D), BF),
            vm((256, D), BF),
            vm((64, D), BF),
            vm((64, D), BF),
            vm((2, 64, D), BF),
            vm((64, D), BF),
            vm((4, ROWS, D), BF),
            vm((COLS, D), BF),
            vm((2 * COLS, D), F32),
            vm((2 * COLS, D), BF),
            vm((COLS, D), F32),
            vm((COLS, D), BF),
            vm((COLS, D), BF),
            vm((COLS, D), BF),
            vm((32, 8, 128), F32),
            vm((8, 512), F32),
            dma((5,)),
            dma((3, NX)),
            dma((3, NX)),
            dma((4, 4)),
            dma((16,)),
            dma((32,)),
            dma,
            dma,
            dma((3, NX)),
            dma((NX,)),
            dma((NX,)),
            dma((NX,)),
            dma((NF,)),
            dma((NF,)),
            dma((3, 2, NF)),
            dma((2, NF)),
            dma((2, 2, NF)),
            dma((4, NF)),
            dma((4, NF)),
        ],
        compiler_params=pltpu.CompilerParams(
            collective_id=0, has_side_effects=True, vmem_limit_bytes=44 * 2**20
        ),
    )(*hbm)
    parts = ((0, ROWS), (ROWS, ROWS), (2 * ROWS, NEG))
    return pl.pallas_call(
        placed,
        out_shape=tuple(pltpu.HBM((n, D), BF) for _, n in parts),
        in_specs=[pl.BlockSpec(memory_space=pltpu.VMEM)],
        scratch_shapes=[dma((3,))],
    )(pltpu.with_memory_space_constraint(out, pltpu.VMEM))


def solution(mesh):
    rows = P(("blk", "grp"), None)
    return jax.shard_map(
        on_device,
        mesh=mesh,
        in_specs=(rows, rows, rows, P(("blk", "grp")), rows),
        out_specs=(rows, rows, rows),
        check_vma=False,
    )
```

```python
import jax
import jax.numpy as jnp
from jax import lax
from jax.experimental import pallas as pl
from jax.experimental.pallas import tpu as pltpu
from jax.sharding import PartitionSpec as P

MESH = pl.DeviceIdType.MESH
BF = jnp.bfloat16
F32 = jnp.float32
INV = 50.0
D = 4096
EXT = 128
NEG = 64
ROWS = 16
COLS = NEG + ROWS
CH = 2048
NF = D // CH
CX = 1024
NX = D // CX
HX = NX // 2
MIX = tuple(f for i in range(HX) for f in (i, i + HX))
GATHER = ((0, 1536), (1536, 512), (2048, 1536), (3584, 512))
FLOOR = -1e30
RETURN = ((0, 512), (512, 1536), (2048, 512), (2560, 1536))


def kernel(
    q_in, p_in, n_in, pos_in, ids_in, out,
    PO, ID, E, Q, C, S, W, MU, sibs, ownq, rsib, G, rB2, gB, rB, T, rA, g3, g12, gsend, g0, rx2, rf1, rf2, st1, MT,
    lsem, sx, rx, sq, ssq, rq, sst, rst1, sg, rg2, rgf1, rgf2, ssib, rsibs, sB, rB2s, rBs, sA, rAs,
):
    b_id = lax.axis_index("blk")
    g_id = lax.axis_index("grp")
    x = b_id % 4
    y = (g_id // 8) * 2 + b_id // 4
    z = (g_id // 2) % 4
    c = g_id % 2

    def dev(xx, yy, zz, cc):
        xx, yy, zz = (xx + 4) % 4, (yy + 4) % 4, (zz + 4) % 4
        return {"blk": (yy % 2) * 4 + xx, "grp": ((yy // 2) * 4 + zz) * 2 + cc}

    right, left, sib = dev(x + 1, y, z, c), dev(x - 1, y, z, c), dev(x, y, z, 1 - c)
    A = z + c * (y - z)
    B = y + c * (z - y)

    def at(a, b):
        a, b = (a + 4) % 4, (b + 4) % 4
        return dev(x, b + c * (a - b), a + c * (b - a), c)

    def slot(cc, b, a):
        return cc * 16 + ((b + 4) % 4) * 4 + (a + 4) % 4

    def rows_of(s, count=ROWS):
        return pl.ds(pl.multiple_of(s * ROWS, ROWS), count)

    sent = []

    def send(src, dst, ss, rs, to):
        cp = pltpu.make_async_remote_copy(
            src_ref=src, dst_ref=dst, send_sem=ss, recv_sem=rs, device_id=to, device_id_type=MESH
        )
        cp.start()
        sent.append(cp)

    def flush():
        for cp in sent:
            cp.wait_send()
        sent.clear()

    def arrived(dst, rs):
        pltpu.make_async_remote_copy(
            src_ref=dst, dst_ref=dst, send_sem=lsem.at[0], recv_sem=rs, device_id=sib, device_id_type=MESH
        ).wait_recv()

    barrier = pltpu.get_barrier_semaphore()
    greet = [right, left, at(A + 2, B), at(A, B + 2), at(A + 1, B), at(A - 1, B), at(A, B + 1), at(A, B - 1), sib]
    for to in greet:
        pl.semaphore_signal(barrier, inc=1, device_id=to, device_id_type=MESH)
    mine = slot(c, B, A)
    own_rows = rows_of(mine)
    local = [
        pltpu.make_async_copy(n_in, C.at[pl.ds(0, NEG)], lsem.at[0]),
        pltpu.make_async_copy(p_in, C.at[pl.ds(NEG, ROWS)], lsem.at[1]),
        pltpu.make_async_copy(q_in, Q.at[own_rows, pl.ds(0, D)], lsem.at[2]),
        pltpu.make_async_copy(pos_in, PO, lsem.at[3]),
        pltpu.make_async_copy(ids_in, ID, lsem.at[4]),
    ]
    for cp in local:
        cp.start()
    local[0].wait()
    local[1].wait()
    pl.semaphore_wait(barrier, len(greet))

    def fcols(f):
        return pl.ds(f * CH, CH)

    def gcols(f):
        return pl.ds(*GATHER[f])

    def scols(f):
        return pl.ds(*RETURN[f])

    def crows(k):
        return pl.ds(k * COLS, COLS)

    for f in range(NX):
        h = (f + HX) % NX
        send(C.at[crows(0), gcols(f)], C.at[crows(1), gcols(f)], sx.at[0, f], rx.at[0, f], right)
        send(C.at[crows(0), gcols(h)], C.at[crows(2), gcols(h)], sx.at[1, h], rx.at[1, h], left)
    E[...] = jnp.zeros((128, 128), F32)
    for cp in local[2:]:
        cp.wait()
    for r, part in ((0, ID[...]), (7, PO[...])):
        n = part.shape[0]
        E[r : r + n, 0:ROWS] = (part // 128).astype(F32)
        E[8 + r : 8 + r + n, 0:ROWS] = (part % 128).astype(F32)
    Q[own_rows, D : D + EXT] = jnp.transpose(E[...])[0:ROWS].astype(BF)
    for da in (1, 3, 2):
        send(Q.at[own_rows], Q.at[own_rows], sq.at[0, da], rq.at[mine], at(A + da, B))

    def to_sib(r, i):
        send(Q.at[rows_of(r)], Q.at[rows_of(r)], ssq.at[i], rq.at[r], sib)

    def spread(da):
        r = slot(c, B, A - da)
        rr = rows_of(r)
        if da:
            arrived(Q.at[rr], rq.at[r])
        for i, db in enumerate((1, -1)):
            send(Q.at[rr], Q.at[rr], sq.at[1 + i, da], rq.at[r], at(A, B + db))
        if da > 1:
            send(Q.at[rr], Q.at[rr], sq.at[3, da], rq.at[r], at(A, B + 2))
        to_sib(r, da)

    def pass_on(da):
        for i, db in enumerate((1, -1)):
            r = slot(c, B - db, A - da)
            rr = rows_of(r)
            arrived(Q.at[rr], rq.at[r])
            if da == i:
                send(Q.at[rr], Q.at[rr], sq.at[3, da], rq.at[r], at(A, B + db))
            to_sib(r, 4 + 4 * i + da)

    def columns_on(f):
        arrived(C.at[crows(1), gcols(f)], rx.at[0, f])
        send(C.at[crows(1), gcols(f)], C.at[crows(3), gcols(f)], sx.at[2, f], rx.at[2, f], right)
        h = f + HX
        arrived(C.at[crows(2), gcols(h)], rx.at[1, h])
        send(C.at[crows(2), gcols(h)], C.at[crows(3), gcols(h)], sx.at[2, h], rx.at[2, h], left)

    for da in (0, 1, 3):
        spread(da)
    pass_on(0)
    spread(2)
    columns_on(0)
    pass_on(1)
    pass_on(3)
    columns_on(1)
    pass_on(2)
    for da in (0, 1, 3, 2):
        r = slot(c, B + 2, A - da)
        arrived(Q.at[rows_of(r)], rq.at[r])
        to_sib(r, 12 + da)
    col_neg = lax.broadcasted_iota(jnp.int32, (NEG, 256), 0)
    col_pas = lax.broadcasted_iota(jnp.int32, (ROWS, 256), 0)

    def dots(lo, hi, rows, d0, d1):
        return INV * lax.dot_general(
            C[lo:hi, d0:d1], Q[rows, d0:d1], (((1,), (1,)), ((), ())), preferred_element_type=F32
        )

    def partial_stats(lo, hi, qs):
        for k in range(lo // COLS, hi // COLS):
            r0, r1 = k * COLS, k * COLS + NEG
            S[r0:r1, qs] = jnp.where(MU[r0:r1, qs] > 0.0, S[r0:r1, qs], FLOOR)
        m = jnp.max(S[lo:hi, qs], 0, keepdims=True)
        tot = jnp.zeros_like(m)
        for k in range(lo // COLS, hi // COLS):
            r0, r1, r2 = k * COLS, k * COLS + NEG, (k + 1) * COLS
            tot = tot + jnp.sum(jnp.exp(S[r0:r1, qs] - m) * MU[r0:r1, qs], 0, keepdims=True)
            tot = tot + jnp.sum(jnp.exp(S[r1:r2, qs] - m), 0, keepdims=True)
        return m, tot

    def half_scores(core):
        qs = pl.ds(pl.multiple_of(core * 256, 256), 256)
        ext = jnp.transpose(Q[qs, D : D + EXT].astype(F32))
        ids = ext[0:8] * 128.0 + ext[8:16]
        for k, dx in enumerate((0, 3, 1, 2)):
            lin = ((y % 2) * 4 + (x + dx) % 4) * 16 + g_id
            gid = (col_neg + lin * NEG).astype(F32)
            mult = jnp.zeros((NEG, 256), F32)
            for h in range(7):
                mult = mult + (ids[h : h + 1] == gid).astype(F32)
            MU[k * COLS : k * COLS + NEG, qs] = mult
            pid = (col_pas + lin * ROWS).astype(F32)
            MU[k * COLS + NEG : (k + 1) * COLS, qs] = (ids[7:8] == pid).astype(F32)
        S[0 : 3 * COLS, qs] = dots(0, 3 * COLS, qs, 0, D)
        m, tot = partial_stats(0, 3 * COLS, qs)
        MT[0:1, qs] = m
        MT[1:2, qs] = tot

    for f in range(HX):
        arrived(C.at[crows(1), gcols(f + HX)], rx.at[0, f + HX])
        arrived(C.at[crows(2), gcols(f)], rx.at[1, f])
    half_scores(c)
    for k in range(16):
        r = (1 - c) * 16 + k
        arrived(Q.at[rows_of(r)], rq.at[r])
    half_scores(1 - c)
    acc = jnp.zeros((COLS, 512), F32)
    for f in MIX:
        arrived(C.at[crows(3), gcols(f)], rx.at[2, f])
        acc = acc + dots(3 * COLS, 4 * COLS, slice(0, 512), GATHER[f][0], sum(GATHER[f]))
    S[3 * COLS : 4 * COLS, :] = acc
    m_b, tot_b = partial_stats(3 * COLS, 4 * COLS, slice(0, 512))
    m_a, tot_a = MT[0:1, :], MT[1:2, :]

    m = jnp.maximum(m_a, m_b)
    tot = tot_a * jnp.exp(m_a - m) + tot_b * jnp.exp(m_b - m)
    for j in range(4):
        st1[0, j : j + 1, :] = m[:, j * 128 : (j + 1) * 128]
        st1[0, 4 + j : 5 + j, :] = tot[:, j * 128 : (j + 1) * 128]

    def merge(buf, n):
        top = buf[0, 0:4, :]
        for i in range(1, n):
            top = jnp.maximum(top, buf[i, 0:4, :])
        total = jnp.zeros((4, 128), F32)
        for i in range(n):
            total = total + buf[i, 4:8, :] * jnp.exp(buf[i, 0:4, :] - top)
        return top, total

    earlier = len(sent)
    def hops(i):
        dy, dz = i // 8, i // 2 % 4
        return min(dy, 4 - dy) + min(dz, 4 - dz)

    for i in sorted(range(1, 32), key=hops, reverse=True):
        dy, dz, dc = i // 8, i // 2 % 4, i % 2
        send(st1.at[0], st1.at[i], sst, rst1, dev(x, y + dy, z + dz, (c + dc) % 2))
    del sent[earlier:]
    flush()
    S[3 * COLS : 4 * COLS, :] = jnp.exp(S[3 * COLS : 4 * COLS, :] - m)
    others = st1.at[pl.ds(1, 31)]
    arrived(others, rst1)
    top, total = merge(st1, 32)
    lt = top + jnp.log(total)
    log_total = jnp.concatenate([lt[j : j + 1, :] for j in range(4)], 1)

    def weights(k):
        r0, r1, r2 = k * COLS, k * COLS + NEG, (k + 1) * COLS
        hard = jnp.exp(S[r0:r1, :] - log_total).astype(BF).astype(F32) * MU[r0:r1, :]
        W[r0:r1, :] = hard.astype(BF)
        W[r1:r2, :] = (jnp.exp(S[r1:r2, :] - log_total) - MU[r1:r2, :]).astype(BF)

    def col_grad(lo, hi, f):
        return INV * jnp.dot(W[lo:hi, :], Q[:, RETURN[f][0] : sum(RETURN[f])], preferred_element_type=F32)

    scale = jnp.exp(m - log_total)
    r0, r1, r2 = 3 * COLS, 3 * COLS + NEG, 4 * COLS
    W[r0:r1, :] = ((S[r0:r1, :] * scale).astype(BF).astype(F32) * MU[r0:r1, :]).astype(BF)
    W[r1:r2, :] = (S[r1:r2, :] * scale - MU[r1:r2, :]).astype(BF)
    for f in MIX:
        g3[:, RETURN[f][0] : sum(RETURN[f])] = col_grad(3 * COLS, 4 * COLS, f).astype(BF)
        to = right if f < HX else left
        send(g3.at[:, scols(f)], rx2.at[:, scols(f)], sg.at[0, f], rg2.at[f], to)
    for k in (0, 1, 2):
        weights(k)

    def query_grad(core, f):
        w = W[:, pl.ds(pl.multiple_of(core * 256, 256), 256)]
        return INV * lax.dot_general(
            w, C[:, f * CH : (f + 1) * CH], (((0,), (0,)), ((), ())), preferred_element_type=F32
        )

    def half(i):
        return pl.ds(32 * i, 32)

    def group(b, i):
        return rows_of(slot(0, b, 2 * i), 32)

    for f in MIX:
        cs = slice(RETURN[f][0], sum(RETURN[f]))
        g12[:, cs] = col_grad(COLS, 3 * COLS, f)
        if f < HX:
            gsend[0:COLS, cs] = g12[0:COLS, cs].astype(BF)
            send(gsend.at[pl.ds(0, COLS), scols(f)], rf2.at[:, scols(f)], sg.at[1, f], rgf2.at[f], left)
        else:
            gsend[COLS:, cs] = g12[COLS:, cs].astype(BF)
            send(gsend.at[pl.ds(COLS, COLS), scols(f)], rf1.at[:, scols(f)], sg.at[1, f], rgf1.at[f], right)
    for f in range(NF):
        sibs[:, f * CH : (f + 1) * CH] = query_grad(1 - c, f).astype(BF)
        send(sibs.at[:, fcols(f)], rsib.at[:, fcols(f)], ssib.at[f], rsibs.at[f], sib)
    for f in range(NF):
        ownq[:, f * CH : (f + 1) * CH] = query_grad(c, f)
    for f in range(NF):
        cs = slice(f * CH, (f + 1) * CH)
        arrived(rsib.at[:, fcols(f)], rsibs.at[f])
        G[:, cs] = (ownq[:, cs] + rsib[:, cs].astype(F32)).astype(BF)
        for i, db in enumerate((1, -1)):
            h, o = half(i), half(1 - i)
            src = G.at[group(B + 2, i), fcols(f)]
            send(src, rB2.at[h, fcols(f)], sB.at[0, i, f], rB2s.at[i, f], at(A, B + db))
            src = G.at[group(B + db, 1 - i), fcols(f)]
            send(src, rB.at[i, o, fcols(f)], sB.at[1, i, f], rBs.at[i, 1 - i, f], at(A, B + db))
    for f in range(NF):
        cs = slice(f * CH, (f + 1) * CH)
        for i, db in enumerate((1, -1)):
            h = half(i)
            arrived(rB2.at[h, fcols(f)], rB2s.at[i, f])
            t = G[group(B + db, i), cs].astype(F32) + rB2[h, cs].astype(F32)
            gB[h, cs] = t.astype(BF)
            send(gB.at[h, fcols(f)], rB.at[i, h, fcols(f)], sB.at[2, i, f], rBs.at[i, i, f], at(A, B + db))
    for f in MIX:
        cs = slice(RETURN[f][0], sum(RETURN[f]))
        arrived(rx2.at[:, scols(f)], rg2.at[f])
        if f < HX:
            gsend[COLS:, cs] = (g12[COLS:, cs] + rx2[:, cs].astype(F32)).astype(BF)
            send(gsend.at[pl.ds(COLS, COLS), scols(f)], rf1.at[:, scols(f)], sg.at[2, f], rgf1.at[f], right)
        else:
            gsend[0:COLS, cs] = (g12[0:COLS, cs] + rx2[:, cs].astype(F32)).astype(BF)
            send(gsend.at[pl.ds(0, COLS), scols(f)], rf2.at[:, scols(f)], sg.at[2, f], rgf2.at[f], left)
    for f in range(NX):
        g0[:, RETURN[f][0] : sum(RETURN[f])] = col_grad(0, COLS, f)
    for f in range(NF):
        cs = slice(f * CH, (f + 1) * CH)
        t = G[rows_of(slot(0, B, 0), 64), cs].astype(F32)
        for i in range(2):
            for j in range(2):
                arrived(rB.at[i, half(j), fcols(f)], rBs.at[i, j, f])
            t = t + rB[i, :, cs].astype(F32)
        T[:, cs] = t.astype(BF)
        for da in (2, 1, 3):
            src = T.at[rows_of(slot(0, 0, A + da)), fcols(f)]
            send(src, rA.at[da, :, fcols(f)], sA.at[da, f], rAs.at[da, f], at(A + da, B))
    flush()
    for f in range(NF):
        cs = slice(f * CH, (f + 1) * CH)
        t = T[rows_of(A), cs].astype(F32)
        for da in (1, 2, 3):
            arrived(rA.at[da, :, fcols(f)], rAs.at[da, f])
            t = t + rA[da, :, cs].astype(F32)
        out[0:ROWS, cs] = t.astype(BF)
    for f in MIX:
        cs = slice(RETURN[f][0], sum(RETURN[f]))
        arrived(rf1.at[:, scols(f)], rgf1.at[f])
        arrived(rf2.at[:, scols(f)], rgf2.at[f])
        t = g0[:, cs] + rf1[:, cs].astype(F32) + rf2[:, cs].astype(F32)
        out[2 * ROWS :, cs] = t[0:NEG].astype(BF)
        out[ROWS : 2 * ROWS, cs] = t[NEG:COLS].astype(BF)
    flush()
    pltpu.make_async_remote_copy(
        src_ref=others, dst_ref=others, send_sem=sst, recv_sem=rst1, device_id=sib, device_id_type=MESH
    ).wait_send()


def placed(held, oq, op, on, sem):
    copies = [
        pltpu.make_async_copy(held.at[pl.ds(0, ROWS)], oq, sem.at[0]),
        pltpu.make_async_copy(held.at[pl.ds(ROWS, ROWS)], op, sem.at[1]),
        pltpu.make_async_copy(held.at[pl.ds(2 * ROWS, NEG)], on, sem.at[2]),
    ]
    for cp in copies:
        cp.start()
    for cp in copies:
        cp.wait()


def on_device(queries, document_vectors, negatives, positives, neg_ids):
    dma = pltpu.SemaphoreType.DMA
    vm = pltpu.VMEM
    hbm = [
        pltpu.with_memory_space_constraint(a, pltpu.HBM)
        for a in (queries, document_vectors, negatives, positives.reshape(1, ROWS), neg_ids.T)
    ]
    out = pl.pallas_call(
        kernel,
        out_shape=pltpu.VMEM((2 * ROWS + NEG, D), BF),
        in_specs=[pl.BlockSpec(memory_space=pltpu.HBM)] * 5,
        scratch_shapes=[
            vm((1, ROWS), jnp.int32),
            vm((7, ROWS), jnp.int32),
            vm((128, 128), F32),
            vm((512, D + EXT), BF),
            vm((4 * COLS, D), BF),
            vm((4 * COLS, 512), F32),
            vm((4 * COLS, 512), BF),
            vm((4 * COLS, 512), F32),
            vm((256, D), BF),
            vm((256, D), F32),
            vm((256, D), BF),
            vm((256, D), BF),
            vm((64, D), BF),
            vm((64, D), BF),
            vm((2, 64, D), BF),
            vm((64, D), BF),
            vm((4, ROWS, D), BF),
            vm((COLS, D), BF),
            vm((2 * COLS, D), F32),
            vm((2 * COLS, D), BF),
            vm((COLS, D), F32),
            vm((COLS, D), BF),
            vm((COLS, D), BF),
            vm((COLS, D), BF),
            vm((32, 8, 128), F32),
            vm((8, 512), F32),
            dma((5,)),
            dma((3, NX)),
            dma((3, NX)),
            dma((4, 4)),
            dma((16,)),
            dma((32,)),
            dma,
            dma,
            dma((3, NX)),
            dma((NX,)),
            dma((NX,)),
            dma((NX,)),
            dma((NF,)),
            dma((NF,)),
            dma((3, 2, NF)),
            dma((2, NF)),
            dma((2, 2, NF)),
            dma((4, NF)),
            dma((4, NF)),
        ],
        compiler_params=pltpu.CompilerParams(
            collective_id=0, has_side_effects=True, vmem_limit_bytes=44 * 2**20
        ),
    )(*hbm)
    parts = ((0, ROWS), (ROWS, ROWS), (2 * ROWS, NEG))
    return pl.pallas_call(
        placed,
        out_shape=tuple(pltpu.HBM((n, D), BF) for _, n in parts),
        in_specs=[pl.BlockSpec(memory_space=pltpu.VMEM)],
        scratch_shapes=[dma((3,))],
    )(pltpu.with_memory_space_constraint(out, pltpu.VMEM))


def solution(mesh):
    rows = P(("blk", "grp"), None)
    return jax.shard_map(
        on_device,
        mesh=mesh,
        in_specs=(rows, rows, rows, P(("blk", "grp")), rows),
        out_specs=(rows, rows, rows),
        check_vma=False,
    )
```
